32 devices in a mesh: strata: 4 (over y, core), chain: 8 (over z, x).
Axes of the slice: x: 2, y: 2, z: 4, core: 2. Of those that a mesh axis runs over, the one named last changes fastest.
Arguments:
- features: bfloat16 [65536, 512], P(('strata', 'chain')), may hold values from -6 to 6
- events: int32 [65536, 35], P(('strata', 'chain')), may hold values from 0 to 32767, as said below
- tie_first: int32 [65536], P(('strata', 'chain')), may hold values from 0 to 16383, as said below
- entry_row: int32 [65536], P(('strata', 'chain')), may hold values from 0 to 16383, as said below
- w_in: bfloat16 [512, 512], replicated, may hold values from -0.25 to 0.25
- w_mid: bfloat16 [512, 512], replicated, may hold values from -0.25 to 0.25
- w_out: bfloat16 [512, 512], replicated, may hold values from -0.25 to 0.25
Outputs:
- endpoint_loss: float32 [512], replicated
- grad_x: bfloat16 [65536, 512], P(('strata', 'chain'))
- grad_in: float32 [512, 512], replicated
- grad_mid: float32 [512, 512], replicated
- grad_out: float32 [512, 512], replicated
The draws below stay inside these ranges and needn't reach their ends.
Inputs may be any that keep to these rules, and one draw needn't show every extreme that they name: Bit b of events[i, k] is row i's event indicator for endpoint 15 k + b; bits 15 and above, and bits for endpoints 512 and beyond, are zero. Groups of equal stop time are runs of consecutive rows lying inside aligned blocks of 2048 rows; tie_first[i] is the first row of row i's run, counted within its stratum. An interval is at risk at the stop time of row k's group exactly when entry_row <= tie_first[k] and the interval's row is >= tie_first[k]. For every row, tie_first[i] - 2048 < entry_row[i] <= tie_first[i]; in every aligned block of 2048 rows some row has entry_row = max(tie_first - 1 * 2048 + 1, 0).
All inputs are finite; a program needn't handle non-finite values.
Results may differ from the reference program's by a relative error of at most 0.006.
The reference program's roundings to bfloat16 on the way (of `first_hidden`, `hidden`, `eta_grad`, `mid_grad` and `pre_grad`) count: a program that leaves them out, or rounds other values in their place, can miss the bound.
Values sent between devices are 32-bit elements; how exact they have to be, the bound alone decides.
No kernel may reach another device: no remote copies, remote signals or barrier semaphores. Data moves between devices by JAX's collectives and lax.ppermute only.
A program may use at most 128 MiB of HBM per device.

```python
from functools import partial
import jax
import jax.numpy as jnp
from jax import lax

FEATURES = 512
HIDDEN_SIZE = 512
ENDPOINTS = 512
BACK = 1
CHAIN_ROWS = 2048
WORDS = 35
STRATA = 4
STRATUM_ROWS = 16384
ROWS = 65536


def tie_groups(key):
    position = jnp.arange(ROWS, dtype=jnp.int32)
    starts = jax.random.randint(jax.random.fold_in(key, 11), (ROWS,), 0, 3) == 0
    starts = jnp.logical_or(starts, position % CHAIN_ROWS == 0)
    marked = jnp.where(starts, position, 0)
    leader = lax.cummax(marked, axis=0)
    return (leader - position // STRATUM_ROWS * STRATUM_ROWS, position)


def draw_tie_first(key, part):
    leader, position = tie_groups(key)
    return leader.astype(jnp.int32)


def draw_entry_row(key, part):
    leader, position = tie_groups(key)
    reach_rows = BACK * CHAIN_ROWS
    first_draw = jax.random.randint(jax.random.fold_in(key, 12), (ROWS,), 0, reach_rows)
    second_draw = jax.random.randint(jax.random.fold_in(key, 17), (ROWS,), 0, reach_rows)
    offset = first_draw * second_draw // reach_rows
    block_count = ROWS // CHAIN_ROWS
    gather_rows = jax.random.randint(jax.random.fold_in(key, 18), (block_count,), CHAIN_ROWS // 2, CHAIN_ROWS)
    block_id = position // CHAIN_ROWS
    earlier_row = jnp.take(gather_rows, jnp.maximum(block_id - 1, 0).astype(jnp.int32))
    inner = leader % CHAIN_ROWS
    usable = jnp.logical_and(leader >= CHAIN_ROWS, earlier_row > inner)
    joined = jax.random.randint(jax.random.fold_in(key, 19), (ROWS,), 0, 4) != 0
    target_row = leader - inner - CHAIN_ROWS + earlier_row
    entry = jnp.where(jnp.logical_and(usable, joined), target_row, jnp.maximum(leader - offset, 0))
    chosen = jax.random.randint(jax.random.fold_in(key, 13), (block_count,), 0, CHAIN_ROWS)
    forced = position % CHAIN_ROWS == jnp.repeat(chosen, CHAIN_ROWS)
    entry = jnp.where(forced, jnp.maximum(leader - reach_rows + 1, 0), entry)
    return entry.astype(jnp.int32)


def draw_events(key, part):
    position = jnp.arange(ROWS, dtype=jnp.int32)[:, None]
    starts = jax.random.randint(jax.random.fold_in(key, 15), (ROWS, ENDPOINTS), 0, 256) == 0
    marked = jnp.where(starts, position, -1000000)
    latest = lax.cummax(marked, axis=0)
    span = jax.random.randint(jax.random.fold_in(key, 16), (1, ENDPOINTS), 96, 224)
    active = position - latest < span
    fired = jax.random.randint(jax.random.fold_in(key, 14), (ROWS, ENDPOINTS), 0, 8) != 0
    event_bits = jnp.logical_and(active, fired).astype(jnp.int32)
    event_bits = jnp.pad(event_bits, ((0, 0), (0, WORDS * 15 - ENDPOINTS)))
    column = jnp.arange(WORDS * 15, dtype=jnp.int32)
    weights = jnp.left_shift(jnp.ones_like(column), column % 15)
    return jnp.sum((event_bits * weights).reshape(ROWS, WORDS, 15), axis=2).astype(jnp.int32)


def level_of(rng, shape, cuts, smallest, high):
    def one(dim, blocks):
        heights = jax.random.uniform(jax.random.fold_in(jax.random.fold_in(rng, 6), dim), (blocks,), jnp.float32, smallest / len(cuts), high / len(cuts))
        return jnp.repeat(jnp.exp(heights), shape[dim] // blocks).reshape((-1,) + (1,) * (len(shape) - dim - 1))

    level = one(*cuts[0])
    for cut in cuts[1:]:
        level = level * one(*cut)
    return level


def normal_values(own_key, dims, deviation, limit, cuts=(), kind=jnp.bfloat16):
    values = deviation * jax.random.normal(own_key, dims, jnp.float32)
    if cuts:
        values = values * level_of(own_key, dims, cuts, -0.22, 0.18)
    return jnp.clip(values, -limit, limit).astype(kind)


def setup_inputs(seed: int = 0) -> dict:
    arg_keys = jax.random.split(jax.random.key(seed), 8)
    features = normal_values(arg_keys[0], (ROWS, FEATURES), 1.0, 6.0, ((0, 32),))
    events = draw_events(jax.random.fold_in(arg_keys[7], 71), 0)
    tie_first = draw_tie_first(jax.random.fold_in(arg_keys[7], 71), 0)
    entry_row = draw_entry_row(jax.random.fold_in(arg_keys[7], 71), 0)
    w_in = normal_values(arg_keys[4], (FEATURES, HIDDEN_SIZE), FEATURES ** -0.5, 0.25)
    w_mid = normal_values(arg_keys[5], (HIDDEN_SIZE, HIDDEN_SIZE), HIDDEN_SIZE ** -0.5, 0.25)
    w_out = normal_values(arg_keys[6], (HIDDEN_SIZE, ENDPOINTS), HIDDEN_SIZE ** -0.5, 0.25)
    return {"features": features, "events": events, "tie_first": tie_first, "entry_row": entry_row, "w_in": w_in, "w_mid": w_mid, "w_out": w_out}


def unpack_events(events, out_width):
    column = jnp.arange(out_width, dtype=jnp.int32)
    spread = jnp.repeat(events, 15, axis=1)[:, :out_width]
    return jnp.bitwise_and(jnp.right_shift(spread, column % 15), 1)


def silu_slope(value):
    sigma = jax.nn.sigmoid(value)
    return sigma * (1.0 + value * (1.0 - sigma))


def stratum_pass(inputs, w_in, w_mid, w_out):
    features, events, tie_first, entry_row = inputs
    preact = jnp.dot(features, w_in, preferred_element_type=jnp.float32)
    first_hidden = jax.nn.silu(preact).astype(jnp.bfloat16)
    mid_pre = jnp.dot(first_hidden, w_mid, preferred_element_type=jnp.float32)
    hidden = jax.nn.silu(mid_pre).astype(jnp.bfloat16)
    log_hazard = jnp.dot(hidden, w_out, preferred_element_type=jnp.float32)
    weight = jnp.exp(log_hazard)
    indicator = unpack_events(events, ENDPOINTS).astype(jnp.float32)
    entered = jax.ops.segment_sum(weight, entry_row, num_segments=STRATUM_ROWS)
    at_risk = lax.cumsum(weight - entered, axis=0, reverse=True) + entered
    divisor = jnp.take(at_risk, tie_first, axis=0)
    loss_terms = jnp.sum(indicator * (jnp.log(divisor) - log_hazard), axis=0)
    hazard = indicator / divisor
    grouped = jax.ops.segment_sum(hazard, tie_first, num_segments=STRATUM_ROWS)
    inclusive = lax.cumsum(grouped, axis=0)
    exclusive = inclusive - grouped
    exposure = inclusive - jnp.take(exclusive, entry_row, axis=0)
    eta_grad = (weight * exposure - indicator).astype(jnp.bfloat16)
    grad_out = jnp.dot(hidden.T, eta_grad, preferred_element_type=jnp.float32)
    hidden_grad = jnp.dot(eta_grad, w_out.T, preferred_element_type=jnp.float32)
    mid_grad = (hidden_grad * silu_slope(mid_pre)).astype(jnp.bfloat16)
    grad_mid = jnp.dot(first_hidden.T, mid_grad, preferred_element_type=jnp.float32)
    first_grad = jnp.dot(mid_grad, w_mid.T, preferred_element_type=jnp.float32)
    pre_grad = (first_grad * silu_slope(preact)).astype(jnp.bfloat16)
    grad_in = jnp.dot(features.T, pre_grad, preferred_element_type=jnp.float32)
    grad_x = jnp.dot(pre_grad, w_in.T, preferred_element_type=jnp.float32).astype(jnp.bfloat16)
    return loss_terms, grad_in, grad_mid, grad_out, grad_x


def reference(features, events, tie_first, entry_row, w_in, w_mid, w_out):
    inputs = (features.reshape(STRATA, STRATUM_ROWS, FEATURES),
              events.reshape(STRATA, STRATUM_ROWS, WORDS),
              tie_first.reshape(STRATA, STRATUM_ROWS),
              entry_row.reshape(STRATA, STRATUM_ROWS))
    loss_terms, grad_in, grad_mid, grad_out, grad_x = lax.map(
        partial(stratum_pass, w_in=w_in, w_mid=w_mid, w_out=w_out), inputs)
    factor = ROWS ** -0.5
    endpoint_loss = jnp.sum(loss_terms, axis=0) / ROWS
    return (endpoint_loss, grad_x.reshape(ROWS, FEATURES),
            jnp.sum(grad_in, axis=0) * factor, jnp.sum(grad_mid, axis=0) * factor,
            jnp.sum(grad_out, axis=0) * factor)
```

```python
from functools import partial

import jax
import jax.numpy as jnp
import numpy as np
from jax import lax
from jax.experimental import pallas as pl
from jax.experimental.pallas import tpu as pltpu
from jax.sharding import PartitionSpec as P

BITS = 15
LANES = 128
TILE = 256
DEPTH = 512
GROUP = 256
VMEM_BYTES = 48 * 1024 * 1024
F32 = jnp.float32
BF16 = jnp.bfloat16
I32 = jnp.int32


def two_parts(value):
    top = value.astype(BF16)
    return top, (value - top.astype(F32)).astype(BF16)


def iota(shape, dim):
    return lax.broadcasted_iota(I32, shape, dim)


def ones_where(mask):
    return jnp.where(mask, 1.0, 0.0).astype(BF16)


def dot(a, b, ca=1, cb=0):
    return lax.dot_general(a, b, (((ca,), (cb,)), ((), ())), preferred_element_type=F32)


def widen(column, width):
    return jnp.concatenate([column] * (width // column.shape[1]), axis=1)


def as_column(row):
    parts = [
        jnp.broadcast_to(row[:, k : k + LANES], (LANES, LANES)).T
        for k in range(0, row.shape[1], LANES)
    ]
    return jnp.concatenate(parts, axis=0)


def whole(shape):
    return pl.BlockSpec(shape, lambda i: (0,) * len(shape))


def rows_of(tile, width):
    return pl.BlockSpec((tile, width), lambda i: (i, 0))


def params():
    return pltpu.CompilerParams(vmem_limit_bytes=VMEM_BYTES)


def rank_entries(entry_ref, first_ref, entry_col, first_col, rank_col, rank_row, send, note, cap):
    rows = entry_ref.shape[1]
    high = rows // LANES
    entry_col[...] = as_column(entry_ref[...])
    first_col[...] = as_column(first_ref[...])
    row = entry_ref[...]
    col = entry_col[...]
    crosses_row = row < 0
    crosses = col < 0
    place_row = row + rows
    place = col + rows
    high_row = ones_where((iota((high, rows), 0) == (place_row >> 7)) & crosses_row)
    lane = iota((rows, LANES), 1)
    low_col = jnp.where((lane == (place & (LANES - 1))) & crosses, 1.0, 0.0)
    high_col = ones_where((lane == (place >> 7)) & crosses)
    present = ones_where(dot(high_row, low_col.astype(BF16)) > 0.5)
    square = (LANES, LANES)
    within = dot(present, ones_where(iota(square, 0) < iota(square, 1)))
    small = (high, high)
    ahead = dot(ones_where(iota(small, 1) < iota(small, 0)), present)
    table = within + jnp.sum(ahead, axis=1, keepdims=True)
    table = jnp.concatenate([table, jnp.zeros((LANES - high, LANES), F32)], axis=0)
    table_high = jnp.floor(table * (1.0 / 256.0))
    table_low = table - 256.0 * table_high
    ones = jnp.ones(square, BF16)
    found_high = dot(high_col, table_high.astype(BF16)) * low_col
    found_low = dot(high_col, table_low.astype(BF16)) * low_col
    rank = 256.0 * dot(found_high.astype(BF16), ones) + dot(found_low.astype(BF16), ones)
    rank_col[...] = jnp.where(crosses, rank.astype(I32), -1)
    for k in range(0, rows, LANES):
        rank_row[:, k : k + LANES] = rank_col[k : k + LANES, :].T[0:8]
    count = jnp.sum(present.astype(F32))
    note[...] = jnp.where(iota(note.shape, 0) == 1, jnp.where(count > cap, 1.0, 0.0), 0.0)
    send[cap:, :] = jnp.zeros((send.shape[0] - cap, send.shape[1]), F32)

    def entries(t, _):
        hit = widen(rank_col[...], GROUP) == iota((rows, GROUP), 1) + t * GROUP
        found = jnp.max(jnp.where(hit, widen(entry_col[...] + rows, GROUP), 0), axis=0, keepdims=True)
        send[pl.ds(cap + t, 1), 0:GROUP] = found.astype(F32)
        return 0

    lax.fori_loop(0, cap // GROUP, entries, 0)


def trunk_kernel(
    cap, entry_ref, first_ref, x_ref, events_ref, low_ref, high_ref, shift_ref, w_in, w_mid, w_out,
    first_hidden, hidden, slope_in, slope_mid, weight_out, indicator_out, weight_top, weight_rest,
    send, note, entry_col, first_col, rank_col, rank_row,
):
    step = pl.program_id(0)
    tile = x_ref.shape[0]

    @pl.when(step == 0)
    def _():
        rank_entries(entry_ref, first_ref, entry_col, first_col, rank_col, rank_row, send, note, cap)

    events = events_ref[...]
    spread = dot((events & 255).astype(F32).astype(BF16), low_ref[...])
    spread = spread + dot((events >> 8).astype(F32).astype(BF16), high_ref[...])
    bits = jnp.bitwise_and(jnp.right_shift(spread.astype(I32), shift_ref[...]), 1)
    indicator = bits.astype(F32)
    indicator_out[...] = indicator.astype(BF16)

    preact = dot(x_ref[...], w_in[...])
    sigma = jax.nn.sigmoid(preact)
    first = (preact * sigma).astype(BF16)
    first_hidden[...] = first
    slope_in[...] = sigma * (1.0 + preact * (1.0 - sigma))
    mid_pre = dot(first, w_mid[...])
    sigma = jax.nn.sigmoid(mid_pre)
    second = (mid_pre * sigma).astype(BF16)
    hidden[...] = second
    slope_mid[...] = sigma * (1.0 + mid_pre * (1.0 - sigma))
    log_hazard = dot(second, w_out[...])
    weight = jnp.exp(log_hazard)
    weight_out[...] = weight
    at = pl.ds(pl.multiple_of(step * tile, tile), tile)
    weight_top[at, :], weight_rest[at, :] = two_parts(weight)
    note[0:1, :] -= jnp.sum(indicator * log_hazard, axis=0, keepdims=True)

    @pl.when(step == pl.num_programs(0) - 1)
    def _():
        rows = rank_row.shape[1]

        def total(t, _):
            hit = ones_where(iota((GROUP, rows), 0) + t * GROUP == rank_row[0:1, :])
            at = pl.ds(pl.multiple_of(t * GROUP, GROUP), GROUP)
            send[at, :] = dot(hit, weight_top[...]) + dot(hit, weight_rest[...])
            return 0

        lax.fori_loop(0, cap // GROUP, total, 0)


def trunk(cap, entry, first, features, events, w_in, w_mid, w_out):
    rows, width = features.shape
    mid = w_in.shape[1]
    wide = w_mid.shape[1]
    out_width = w_out.shape[1]
    words = events.shape[1]
    column = np.arange(out_width)
    owner = (np.arange(words)[:, None] == column // BITS).astype(np.float32)
    bit = column % BITS
    low = jnp.asarray(owner * (bit < 8), BF16)
    high = jnp.asarray(owner * (bit >= 8), BF16)
    shift = jnp.asarray((bit % 8)[None, :], I32)
    sent_rows = cap + -(-(cap // GROUP) // 8) * 8
    like = jax.ShapeDtypeStruct
    return pl.pallas_call(
        partial(trunk_kernel, cap),
        grid=(rows // TILE,),
        in_specs=[
            whole((1, rows)), whole((1, rows)), rows_of(TILE, width), rows_of(TILE, words),
            whole((words, out_width)), whole((words, out_width)), whole((1, out_width)),
            whole(w_in.shape), whole(w_mid.shape), whole(w_out.shape),
        ],
        out_specs=[
            rows_of(TILE, mid), rows_of(TILE, wide), rows_of(TILE, mid), rows_of(TILE, wide),
            rows_of(TILE, out_width), rows_of(TILE, out_width), whole((rows, out_width)),
            whole((rows, out_width)), whole((sent_rows, out_width)), whole((8, out_width)),
            whole((rows, LANES)), whole((rows, LANES)), whole((rows, LANES)),
        ],
        out_shape=[
            like((rows, mid), BF16), like((rows, wide), BF16),
            like((rows, mid), F32), like((rows, wide), F32),
            like((rows, out_width), F32), like((rows, out_width), BF16),
            like((rows, out_width), BF16), like((rows, out_width), BF16), like((sent_rows, out_width), F32),
            like((8, out_width), F32), like((rows, LANES), I32),
            like((rows, LANES), I32), like((rows, LANES), I32),
        ],
        scratch_shapes=[pltpu.VMEM((8, rows), I32)],
        compiler_params=params(),
        name="trunk",
    )(entry, first, features, events, low, high, shift, w_in, w_mid, w_out)


def own_risk_kernel(starts, entry_ref, first_col, weight_top, weight_rest, out):
    step = pl.program_id(0)
    tile = out.shape[0]
    rows = weight_top.shape[0]
    first = widen(first_col[...], DEPTH)
    out[...] = jnp.zeros_like(out)

    def part(k, _):
        at = pl.multiple_of(k * DEPTH, DEPTH)
        row = iota((tile, DEPTH), 1) + at
        entry = entry_ref[pl.ds(k, 1), :]
        mask = ones_where((row >= first) & (entry <= first))
        at = pl.ds(at, DEPTH)
        out[...] += dot(mask, weight_top[at, :]) + dot(mask, weight_rest[at, :])
        return 0

    lax.fori_loop(starts[step] // DEPTH, rows // DEPTH, part, 0)


def own_risk(starts, entry, first_col, weight_top, weight_rest):
    rows, width = weight_top.shape
    split = entry.reshape(rows // DEPTH, DEPTH)
    return pl.pallas_call(
        own_risk_kernel,
        grid_spec=pltpu.PrefetchScalarGridSpec(
            num_scalar_prefetch=1,
            grid=(rows // TILE,),
            in_specs=[
                pl.BlockSpec(split.shape, lambda i, s: (0, 0)),
                pl.BlockSpec((TILE, LANES), lambda i, s: (i, 0)),
                pl.BlockSpec((rows, width), lambda i, s: (0, 0)),
                pl.BlockSpec((rows, width), lambda i, s: (0, 0)),
            ],
            out_specs=pl.BlockSpec((TILE, width), lambda i, s: (i, 0)),
        ),
        out_shape=jax.ShapeDtypeStruct((rows, width), F32),
        compiler_params=params(),
        cost_estimate=pl.CostEstimate(
            flops=rows * rows * width * 2, bytes_accessed=rows * width * 8, transcendentals=0
        ),
        name="own_risk",
    )(starts, split, first_col, weight_top, weight_rest)


def own_exposure_kernel(starts, first_ref, entry_col, hazard_top, hazard_rest, out):
    step = pl.program_id(0)
    tile = out.shape[0]
    entry = widen(entry_col[...], DEPTH)
    row = iota((tile, DEPTH), 0) + step * tile
    out[...] = jnp.zeros_like(out)
    last = step * tile + tile - 1
    parts = jnp.int32(0)
    per = DEPTH // tile
    for k in range(first_ref.shape[0]):
        parts += jnp.where(starts[k * per] <= last, 1, 0).astype(I32)

    def part(k, _):
        at = pl.multiple_of(k * DEPTH, DEPTH)
        first = first_ref[pl.ds(k, 1), :]
        mask = ones_where((first >= entry) & (first <= row))
        at = pl.ds(at, DEPTH)
        out[...] += dot(mask, hazard_top[at, :]) + dot(mask, hazard_rest[at, :])
        return 0

    lax.fori_loop(0, parts, part, 0)


def own_exposure(starts, first, entry_col, hazard_top, hazard_rest):
    rows, width = hazard_top.shape
    split = first.reshape(rows // DEPTH, DEPTH)
    return pl.pallas_call(
        own_exposure_kernel,
        grid_spec=pltpu.PrefetchScalarGridSpec(
            num_scalar_prefetch=1,
            grid=(rows // TILE,),
            in_specs=[
                pl.BlockSpec(split.shape, lambda i, s: (0, 0)),
                pl.BlockSpec((TILE, LANES), lambda i, s: (i, 0)),
                pl.BlockSpec((rows, width), lambda i, s: (0, 0)),
                pl.BlockSpec((rows, width), lambda i, s: (0, 0)),
            ],
            out_specs=pl.BlockSpec((TILE, width), lambda i, s: (i, 0)),
        ),
        out_shape=jax.ShapeDtypeStruct((rows, width), F32),
        compiler_params=params(),
        cost_estimate=pl.CostEstimate(
            flops=rows * rows * width * 2, bytes_accessed=rows * width * 8, transcendentals=0
        ),
        name="own_exposure",
    )(starts, split, entry_col, hazard_top, hazard_rest)


def split_sum(source, high, low, cap):
    for t in range(0, cap, GROUP):
        high[t : t + GROUP, :], low[t : t + GROUP, :] = two_parts(source[t : t + GROUP, :])


def hazard_kernel(
    cap, first_ref, first_col, risk, indicator_ref, got, hazard_top, hazard_rest,
    sums, note, high, low,
):
    step = pl.program_id(0)
    tile = risk.shape[0]
    rows = hazard_top.shape[0]

    @pl.when(step == 0)
    def _():
        split_sum(got, high, low, cap)
        note[...] = jnp.zeros_like(note)

    first = widen(first_col[...].astype(F32), GROUP)
    divisor = risk[...]

    def beyond(t, total):
        entry = got[pl.ds(cap + t, 1), 0:GROUP]
        mask = ones_where(entry <= first)
        at = pl.ds(pl.multiple_of(t * GROUP, GROUP), GROUP)
        return total + dot(mask, high[at, :]) + dot(mask, low[at, :])

    divisor = lax.fori_loop(0, cap // GROUP, beyond, divisor)
    indicator = indicator_ref[...].astype(F32)
    note[0:1, :] += jnp.sum(indicator * jnp.log(divisor), axis=0, keepdims=True)
    at = pl.ds(pl.multiple_of(step * tile, tile), tile)
    hazard_top[at, :], hazard_rest[at, :] = two_parts(indicator / divisor)

    @pl.when(step == pl.num_programs(0) - 1)
    def _():
        def total(t, _):
            entry = widen(as_column(got[pl.ds(cap + t, 1), 0:GROUP]), rows)
            mask = ones_where(first_ref[...].astype(F32) >= entry)
            at = pl.ds(pl.multiple_of(t * GROUP, GROUP), GROUP)
            sums[at, :] = dot(mask, hazard_top[...]) + dot(mask, hazard_rest[...])
            return 0

        lax.fori_loop(0, cap // GROUP, total, 0)


def hazards(cap, first, first_col, risk, indicator, got):
    rows, width = risk.shape
    like = jax.ShapeDtypeStruct
    return pl.pallas_call(
        partial(hazard_kernel, cap),
        grid=(rows // TILE,),
        in_specs=[
            whole((1, rows)), rows_of(TILE, LANES), rows_of(TILE, width), rows_of(TILE, width),
            whole(got.shape),
        ],
        out_specs=[
            whole((rows, width)), whole((rows, width)), whole((cap, width)), whole((8, width)),
        ],
        out_shape=[
            like((rows, width), BF16), like((rows, width), BF16),
            like((cap, width), F32), like((8, width), F32),
        ],
        scratch_shapes=[pltpu.VMEM((cap, width), BF16), pltpu.VMEM((cap, width), BF16)],
        compiler_params=params(),
        name="hazards",
    )(first, first_col, risk, indicator, got)


def backward_kernel(
    cap, factor, rank_col, exposure_ref, got, weight, indicator, hidden, slope_mid, first_hidden,
    slope_in, x_ref, w_in, w_mid, w_out, grad_x, grad_in, grad_mid, grad_out, high, low,
):
    step = pl.program_id(0)
    tile = weight.shape[0]

    @pl.when(step == 0)
    def _():
        split_sum(got, high, low, cap)
        grad_in[...] = jnp.zeros_like(grad_in)
        grad_mid[...] = jnp.zeros_like(grad_mid)
        grad_out[...] = jnp.zeros_like(grad_out)

    rank = widen(rank_col[...], GROUP)

    def behind(t, total):
        mask = ones_where(rank == iota((tile, GROUP), 1) + t * GROUP)
        at = pl.ds(pl.multiple_of(t * GROUP, GROUP), GROUP)
        return total + dot(mask, high[at, :]) + dot(mask, low[at, :])

    exposure = lax.fori_loop(0, cap // GROUP, behind, exposure_ref[...])
    eta = (weight[...] * exposure - indicator[...].astype(F32)).astype(BF16)
    grad_out[...] += dot(hidden[...], eta, 0, 0)
    mid = (dot(eta, w_out[...], 1, 1) * slope_mid[...]).astype(BF16)
    grad_mid[...] += dot(first_hidden[...], mid, 0, 0)
    pre = (dot(mid, w_mid[...], 1, 1) * slope_in[...]).astype(BF16)
    grad_in[...] += dot(x_ref[...], pre, 0, 0)
    grad_x[...] = dot(pre, w_in[...], 1, 1).astype(BF16)

    @pl.when(step == pl.num_programs(0) - 1)
    def _():
        grad_in[...] = grad_in[...] * factor
        grad_mid[...] = grad_mid[...] * factor
        grad_out[...] = grad_out[...] * factor


def backward(cap, factor, rank_col, exposure, got, kept, features, w_in, w_mid, w_out):
    weight, indicator, hidden, slope_mid, first_hidden, slope_in = kept
    rows, width = features.shape
    out_width = weight.shape[1]
    like = jax.ShapeDtypeStruct
    tiles = (weight, indicator, hidden, slope_mid, first_hidden, slope_in, features)
    return pl.pallas_call(
        partial(backward_kernel, cap, factor),
        grid=(rows // TILE,),
        in_specs=[rows_of(TILE, LANES), rows_of(TILE, out_width), whole(got.shape)]
        + [rows_of(TILE, a.shape[1]) for a in tiles]
        + [whole(w.shape) for w in (w_in, w_mid, w_out)],
        out_specs=[rows_of(TILE, width), whole(w_in.shape), whole(w_mid.shape), whole(w_out.shape)],
        out_shape=[like((rows, width), BF16)] + [like(w.shape, F32) for w in (w_in, w_mid, w_out)],
        scratch_shapes=[pltpu.VMEM((cap, out_width), BF16), pltpu.VMEM((cap, out_width), BF16)],
        compiler_params=params(),
        name="backward",
    )(rank_col, exposure, got, *tiles, w_in, w_mid, w_out)


def from_behind(block, axis, distance):
    devices = range(lax.axis_size(axis))
    route = [(i - distance, i) for i in devices if i - distance in devices]
    return lax.ppermute(block, axis, route)


def pipeline(cap, total_rows, features, events, first, entry, w_in, w_mid, w_out):
    rows = features.shape[0]
    first_row = first.reshape(1, rows)
    entry_row = entry.reshape(1, rows)
    starts = first[::TILE]
    (
        first_hidden, hidden, slope_in, slope_mid, weight, indicator, weight_top, weight_rest,
        send, note, entry_col, first_col, rank_col,
    ) = trunk(cap, entry_row, first_row, features, events, w_in, w_mid, w_out)
    got = from_behind(send, "chain", -1)
    risk = own_risk(starts, entry, first_col, weight_top, weight_rest)
    hazard_top, hazard_rest, sums, log_part = hazards(cap, first_row, first_col, risk, indicator, got)
    got_sums = from_behind(sums, "chain", 1)
    exposure = own_exposure(starts, first, entry_col, hazard_top, hazard_rest)
    kept = (weight, indicator, hidden, slope_mid, first_hidden, slope_in)
    factor = total_rows ** (-0.5)
    grads = backward(
        cap, factor, rank_col, exposure, got_sums, kept, features, w_in, w_mid, w_out
    )
    return grads, note + log_part


def on_device(features, events, tie_first, entry_row, w_in, w_mid, w_out):
    rows = features.shape[0]
    total_rows = rows * lax.axis_size("chain") * lax.axis_size("strata")
    block_start = lax.axis_index("chain") * rows
    first = tie_first - block_start
    entry = entry_row - block_start
    args = (features, events, first, entry, w_in, w_mid, w_out)

    def run(cap):
        (grad_x, grad_in, grad_mid, grad_out), note = pipeline(cap, total_rows, *args)
        grad_in, grad_mid, grad_out, note = lax.psum(
            (grad_in, grad_mid, grad_out, note), ("strata", "chain")
        )
        return note[1, 0], (note[0] / total_rows, grad_x, grad_in, grad_mid, grad_out)

    over, out = run(min(GROUP, rows))
    return lax.cond(over > 0, lambda _: run(rows)[1], lambda kept: kept, out)


def solution(mesh):
    placed = (
        P(("strata", "chain"), None),
        P(("strata", "chain"), None),
        P(("strata", "chain")),
        P(("strata", "chain")),
        P(),
        P(),
        P(),
    )
    return jax.shard_map(
        on_device,
        mesh=mesh,
        in_specs=placed,
        out_specs=(P(), P(("strata", "chain"), None), P(), P(), P()),
        check_vma=False,
    )
```

```python
from functools import partial

import jax
import jax.numpy as jnp
import numpy as np
from jax import lax
from jax.experimental import pallas as pl
from jax.experimental.pallas import tpu as pltpu
from jax.sharding import PartitionSpec as P

BITS = 15
LANES = 128
TILE = 512
DEPTH = 512
GROUP = 256
MIB = 1024 * 1024
F32 = jnp.float32
BF16 = jnp.bfloat16
I32 = jnp.int32


def two_parts(value):
    top = value.astype(BF16)
    return top, (value - top.astype(F32)).astype(BF16)


def iota(shape, dim):
    return lax.broadcasted_iota(I32, shape, dim)


def ones_where(mask):
    return jnp.where(mask, 1.0, 0.0).astype(BF16)


def dot(a, b, ca=1, cb=0):
    return lax.dot_general(a, b, (((ca,), (cb,)), ((), ())), preferred_element_type=F32)


def widen(column, width):
    return jnp.concatenate([column] * (width // column.shape[1]), axis=1)


def as_column(row):
    parts = [
        jnp.broadcast_to(row[:, k : k + LANES], (LANES, LANES)).T
        for k in range(0, row.shape[1], LANES)
    ]
    return jnp.concatenate(parts, axis=0)


def whole():
    return pl.BlockSpec(memory_space=pltpu.VMEM)


def rows_of(tile, width):
    return pl.BlockSpec((tile, width), lambda i: (i, 0))


def lanes_of(height, tile):
    return pl.BlockSpec((height, tile), lambda i: (0, i))


def in_hbm(array):
    return pltpu.with_memory_space_constraint(array, pltpu.HBM)


def params(mib):
    return pltpu.CompilerParams(vmem_limit_bytes=mib * MIB)


def rank_entries(entry_ref, rank_ref, note, cap):
    rows = entry_ref.shape[1]
    high = rows // LANES
    place = entry_ref[...] + rows
    crosses = place < rows
    high_hit = ones_where((iota((high, rows), 0) == (place >> 7)) & crosses)
    low_hit = jnp.where((iota((LANES, rows), 0) == (place & (LANES - 1))) & crosses, 1.0, 0.0)
    present = ones_where(dot(high_hit, low_hit.astype(BF16), 1, 1) > 0.5)
    square = (LANES, LANES)
    within = dot(present, ones_where(iota(square, 0) < iota(square, 1)))
    small = (high, high)
    ahead = dot(ones_where(iota(small, 1) < iota(small, 0)), present)
    table = within + jnp.sum(ahead, axis=1, keepdims=True)
    table_high = jnp.floor(table * (1.0 / 256.0))
    table_low = table - 256.0 * table_high
    found = 256.0 * dot(table_high.astype(BF16), high_hit, 0, 0)
    found = found + dot(table_low.astype(BF16), high_hit, 0, 0)
    rank = jnp.sum(found * low_hit, axis=0, keepdims=True)
    rank_ref[...] = jnp.where(crosses, rank.astype(I32), -1)
    count = jnp.sum(present.astype(F32))
    note[...] = jnp.where(iota(note.shape, 0) == 1, jnp.where(count > cap, 1.0, 0.0), 0.0)


def trunk_kernel(
    cap, entry_ref, x_ref, events_ref, low_ref, high_ref, shift_ref, w_in, w_mid, w_out,
    first_hidden, hidden, slope_in, slope_mid, indicator_out, weight_out, weight_top, weight_rest,
    send, note, rank_ref,
):
    step = pl.program_id(0)
    tile = x_ref.shape[0]

    @pl.when(step == 0)
    def _():
        rank_entries(entry_ref, rank_ref, note, cap)

    at = pl.ds(pl.multiple_of(step * tile, tile), tile)
    events = events_ref[...]
    spread = dot((events & 255).astype(F32).astype(BF16), low_ref[...], 0, 0)
    spread = spread + dot((events >> 8).astype(F32).astype(BF16), high_ref[...], 0, 0)
    bits = jnp.bitwise_and(jnp.right_shift(spread.astype(I32), shift_ref[...]), 1)
    indicator = bits.astype(F32)
    indicator_out[...] = indicator.astype(BF16)

    preact = dot(x_ref[...], w_in[...])
    sigma = jax.nn.sigmoid(preact)
    first = (preact * sigma).astype(BF16)
    first_hidden[...] = first
    slope_in[...] = sigma * (1.0 + preact * (1.0 - sigma))
    mid_pre = dot(first, w_mid[...])
    sigma = jax.nn.sigmoid(mid_pre)
    second = (mid_pre * sigma).astype(BF16)
    hidden[...] = second
    slope_mid[...] = sigma * (1.0 + mid_pre * (1.0 - sigma))
    log_hazard = dot(second, w_out[...])
    weight = jnp.exp(log_hazard)
    weight_out[...] = weight
    weight_top[at, :], weight_rest[at, :] = two_parts(weight)
    note[0:1, :] -= jnp.sum(indicator * log_hazard, axis=0, keepdims=True)

    @pl.when(step == pl.num_programs(0) - 1)
    def _():
        rows = rank_ref.shape[1]
        send[cap:, :] = jnp.zeros((send.shape[0] - cap, send.shape[1]), F32)

        def total(t, _):
            hit = iota((GROUP, rows), 0) + t * GROUP == rank_ref[...]
            place = jnp.where(hit, (entry_ref[...] + rows).astype(F32), 0.0)
            place = jnp.max(place, axis=1, keepdims=True)
            place = jnp.broadcast_to(place, (GROUP, LANES))
            parts = [place[k : k + LANES, :].T[0:1] for k in range(0, GROUP, LANES)]
            spot = (send.shape[0] - cap, GROUP)
            place = jnp.broadcast_to(jnp.concatenate(parts, axis=1), spot)
            send[cap:, 0:GROUP] = jnp.where(iota(spot, 0) == t, place, send[cap:, 0:GROUP])
            hit = ones_where(hit)
            at = pl.ds(pl.multiple_of(t * GROUP, GROUP), GROUP)
            send[at, :] = dot(hit, weight_top[...]) + dot(hit, weight_rest[...])
            return 0

        lax.fori_loop(0, cap // GROUP, total, 0)


def trunk(cap, entry, features, events, w_in, w_mid, w_out):
    rows, width = features.shape
    mid = w_in.shape[1]
    wide = w_mid.shape[1]
    out_width = w_out.shape[1]
    words = events.shape[1]
    column = np.arange(out_width)
    owner = (np.arange(words)[:, None] == column // BITS).astype(np.float32)
    bit = column % BITS
    low = jnp.asarray(owner * (bit < 8), BF16)
    high = jnp.asarray(owner * (bit >= 8), BF16)
    shift = jnp.asarray((bit % 8)[None, :], I32)
    sent_rows = cap + -(-(cap // GROUP) // 8) * 8
    like = jax.ShapeDtypeStruct
    return pl.pallas_call(
        partial(trunk_kernel, cap),
        grid=(rows // TILE,),
        in_specs=[whole(), rows_of(TILE, width), lanes_of(words, TILE)] + [whole()] * 6,
        out_specs=[
            rows_of(TILE, mid), rows_of(TILE, wide), rows_of(TILE, mid), rows_of(TILE, wide),
            rows_of(TILE, out_width), rows_of(TILE, out_width),
        ]
        + [whole()] * 5,
        out_shape=[
            pltpu.HBM((rows, mid), BF16), pltpu.HBM((rows, wide), BF16),
            pltpu.HBM((rows, mid), F32), pltpu.HBM((rows, wide), F32),
            pltpu.HBM((rows, out_width), BF16), pltpu.HBM((rows, out_width), F32),
            like((rows, out_width), BF16), like((rows, out_width), BF16), like((sent_rows, out_width), F32),
            like((8, out_width), F32), like((1, rows), I32),
        ],
        compiler_params=params(28),
        name="trunk",
    )(entry, features, events.T, low, high, shift, w_in, w_mid, w_out)


def own_risk_kernel(starts, entry_ref, first_ref, weight_top, weight_rest, out):
    step = pl.program_id(0)
    tile = first_ref.shape[1]
    rows = weight_top.shape[0]
    first = widen(as_column(first_ref[...]), DEPTH)
    own = pl.ds(pl.multiple_of(step * tile, tile), tile)
    out[own, :] = jnp.zeros((tile, out.shape[1]), F32)

    def part(k, _):
        at = pl.multiple_of(k * DEPTH, DEPTH)
        row = iota((tile, DEPTH), 1) + at
        entry = entry_ref[pl.ds(k, 1), :]
        mask = ones_where((row >= first) & (entry <= first))
        at = pl.ds(at, DEPTH)
        out[own, :] += dot(mask, weight_top[at, :]) + dot(mask, weight_rest[at, :])
        return 0

    lax.fori_loop(starts[step] // DEPTH, rows // DEPTH, part, 0)


def block_sum(flops):
    return pl.CostEstimate(flops=flops, bytes_accessed=flops // 256, transcendentals=0)


def own_risk(starts, entry, first, weight_top, weight_rest):
    rows, width = weight_top.shape
    return pl.pallas_call(
        own_risk_kernel,
        grid=(rows // TILE,),
        in_specs=[
            pl.BlockSpec(memory_space=pltpu.SMEM), whole(), lanes_of(1, TILE), whole(), whole()
        ],
        out_specs=whole(),
        out_shape=jax.ShapeDtypeStruct((rows, width), F32),
        compiler_params=params(12),
        cost_estimate=block_sum(rows * rows * width * 4),
        name="own_risk",
    )(starts, entry.reshape(rows // DEPTH, DEPTH), first, weight_top, weight_rest)


def own_exposure_kernel(starts, first_ref, entry_ref, hazard_top, hazard_rest, out, note):
    step = pl.program_id(0)
    tile = entry_ref.shape[1]

    @pl.when(step == 0)
    def _():
        note[...] = jnp.zeros_like(note)

    entry = widen(as_column(entry_ref[...]), DEPTH)
    row = iota((tile, DEPTH), 0) + step * tile
    own = pl.ds(pl.multiple_of(step * tile, tile), tile)
    out[own, :] = jnp.zeros((tile, out.shape[1]), F32)
    last = step * tile + tile - 1
    parts = jnp.int32(0)
    for k in range(first_ref.shape[0]):
        parts += jnp.where(starts[k * (DEPTH // TILE)] <= last, 1, 0).astype(I32)

    def part(k, _):
        at = pl.multiple_of(k * DEPTH, DEPTH)
        first = first_ref[pl.ds(k, 1), :]
        mask = ones_where((first >= entry) & (first <= row))
        at = pl.ds(at, DEPTH)
        out[own, :] += dot(mask, hazard_top[at, :]) + dot(mask, hazard_rest[at, :])
        return 0

    lax.fori_loop(0, parts, part, 0)
    hazard = hazard_top[own, :].astype(F32) + hazard_rest[own, :].astype(F32)
    logs = jnp.where(hazard > 0.0, jnp.log(hazard), 0.0)
    note[0:1, :] -= jnp.sum(logs, axis=0, keepdims=True)


def own_exposure(starts, first, entry, hazard_top, hazard_rest):
    rows, width = hazard_top.shape
    like = jax.ShapeDtypeStruct
    return pl.pallas_call(
        own_exposure_kernel,
        grid=(rows // TILE,),
        in_specs=[
            pl.BlockSpec(memory_space=pltpu.SMEM), whole(), lanes_of(1, TILE), whole(), whole()
        ],
        out_specs=[whole(), whole()],
        out_shape=[like((rows, width), F32), like((8, width), F32)],
        compiler_params=params(12),
        cost_estimate=block_sum(rows * rows * width * 4),
        name="own_exposure",
    )(starts, first.reshape(rows // DEPTH, DEPTH), entry, hazard_top, hazard_rest)


def split_sum(source, high, low, cap):
    for t in range(0, cap, GROUP):
        high[t : t + GROUP, :], low[t : t + GROUP, :] = two_parts(source[t : t + GROUP, :])


def hazard_kernel(
    cap, first_all, first_ref, risk, indicator_ref, got, hazard_top, hazard_rest, sums, high, low
):
    step = pl.program_id(0)
    tile = first_ref.shape[1]
    rows = hazard_top.shape[0]
    own = pl.ds(pl.multiple_of(step * tile, tile), tile)

    @pl.when(step == 0)
    def _():
        split_sum(got, high, low, cap)

    first = widen(as_column(first_ref[...]).astype(F32), GROUP)
    divisor = risk[own, :]

    def beyond(t, total):
        entry = got[pl.ds(cap + t, 1), 0:GROUP]
        mask = ones_where(entry <= first)
        at = pl.ds(pl.multiple_of(t * GROUP, GROUP), GROUP)
        return total + dot(mask, high[at, :]) + dot(mask, low[at, :])

    divisor = lax.fori_loop(0, cap // GROUP, beyond, divisor)
    hazard = indicator_ref[...].astype(F32) / divisor
    hazard_top[own, :], hazard_rest[own, :] = two_parts(hazard)

    @pl.when(step == pl.num_programs(0) - 1)
    def _():
        def total(t, _):
            entry = widen(as_column(got[pl.ds(cap + t, 1), 0:GROUP]), rows)
            mask = ones_where(first_all[...].astype(F32) >= entry)
            at = pl.ds(pl.multiple_of(t * GROUP, GROUP), GROUP)
            sums[at, :] = dot(mask, hazard_top[...]) + dot(mask, hazard_rest[...])
            return 0

        lax.fori_loop(0, cap // GROUP, total, 0)


def hazards(cap, first, risk, indicator, got):
    rows, width = risk.shape
    like = jax.ShapeDtypeStruct
    return pl.pallas_call(
        partial(hazard_kernel, cap),
        grid=(rows // TILE,),
        in_specs=[
            whole(), lanes_of(1, TILE), whole(), rows_of(TILE, width), whole()
        ],
        out_specs=[whole(), whole(), whole()],
        out_shape=[
            like((rows, width), BF16), like((rows, width), BF16), like((cap, width), F32)
        ],
        scratch_shapes=[pltpu.VMEM((cap, width), BF16), pltpu.VMEM((cap, width), BF16)],
        compiler_params=params(20),
        name="hazards",
    )(first, first, risk, in_hbm(indicator), got)


def backward_kernel(
    cap, factor, half, rank_ref, exposure_ref, got, note, log_part, weight, indicator, hidden, slope_mid, first_hidden, slope_in, x_ref, w_in, w_mid, w_out, grad_x, keep, send,
    high, low, grad_in, grad_mid, grad_out,
):
    step = pl.program_id(0)
    tile = rank_ref.shape[1]
    own = pl.ds(pl.multiple_of(step * tile, tile), tile)

    @pl.when(step == 0)
    def _():
        split_sum(got, high, low, cap)
        grad_in[...] = jnp.zeros_like(grad_in)
        grad_mid[...] = jnp.zeros_like(grad_mid)
        grad_out[...] = jnp.zeros_like(grad_out)

    rank = widen(as_column(rank_ref[...]), GROUP)

    def behind(t, total):
        mask = ones_where(rank == iota((tile, GROUP), 1) + t * GROUP)
        at = pl.ds(pl.multiple_of(t * GROUP, GROUP), GROUP)
        return total + dot(mask, high[at, :]) + dot(mask, low[at, :])

    exposure = lax.fori_loop(0, cap // GROUP, behind, exposure_ref[own, :])
    eta = (weight[...] * exposure - indicator[...].astype(F32)).astype(BF16)
    grad_out[...] += dot(hidden[...], eta, 0, 0)
    mid = (dot(eta, w_out[...], 1, 1) * slope_mid[...]).astype(BF16)
    grad_mid[...] += dot(first_hidden[...], mid, 0, 0)
    pre = (dot(mid, w_mid[...], 1, 1) * slope_in[...]).astype(BF16)
    grad_in[...] += dot(x_ref[...], pre, 0, 0)
    grad_x[...] = dot(pre, w_in[...], 1, 1).astype(BF16)

    @pl.when(step == pl.num_programs(0) - 1)
    def _():
        body, rest = grad_mid.shape[0], grad_out.shape[0] // 2
        end = body + rest

        def write(out, block, at):
            out[0:body, :] = block[...] * factor
            out[body:end, :] = grad_out[at : at + rest, :] * factor
            out[end:, :] = note[...] + log_part[...]

        @pl.when(half[0] == 0)
        def _():
            write(keep, grad_mid, 0)
            write(send, grad_in, rest)

        @pl.when(half[0] != 0)
        def _():
            write(keep, grad_in, rest)
            write(send, grad_mid, 0)


def backward(cap, factor, half, rank, exposure, got, notes, kept, features, w_in, w_mid, w_out):
    rows, width = features.shape
    out_width = exposure.shape[1]
    like = jax.ShapeDtypeStruct
    tiles = [in_hbm(a) for a in (*kept, features)]
    weights = (w_in, w_mid, w_out)
    halves = (w_mid.shape[0] + w_out.shape[0] // 2 + 8, out_width)
    return pl.pallas_call(
        partial(backward_kernel, cap, factor),
        grid=(rows // TILE,),
        in_specs=[pl.BlockSpec(memory_space=pltpu.SMEM)]
        + [lanes_of(1, TILE)]
        + [whole()] * (2 + len(notes))
        + [rows_of(TILE, a.shape[1]) for a in tiles]
        + [whole()] * len(weights),
        out_specs=[rows_of(TILE, width), whole(), whole()],
        out_shape=[
            pltpu.HBM((rows, width), BF16), pltpu.HBM(halves, F32), like(halves, F32)
        ],
        scratch_shapes=[pltpu.VMEM((cap, out_width), BF16), pltpu.VMEM((cap, out_width), BF16)]
        + [pltpu.VMEM(w.shape, F32) for w in weights],
        compiler_params=params(28),
        name="backward",
    )(half, rank, exposure, got, *notes, *tiles, *weights)


def spread_kernel(sizes, streams, me, *refs):
    count = sum(sizes)
    outs = iter(refs[count : len(refs) - len(sizes)])
    totals = refs[len(refs) - len(sizes) :]
    start = 0
    for size, total in zip(sizes, totals):
        value = refs[start][...]
        for ref in refs[start + 1 : start + size]:
            value = value + ref[...]
        total[...] = value
        start += size
    for i, (which, at, rows, tail_at, tail, groups) in enumerate(streams):
        total, piece = totals[which], rows // groups
        for m in range(groups):
            out = next(outs)
            begin = pl.multiple_of(at + jnp.bitwise_xor(me[i], m) * piece, 8)
            out[0:piece, :] = total[pl.ds(begin, piece), :]
            if tail:
                out[piece : piece + tail, :] = total[tail_at : tail_at + tail, :]


def spread(terms, streams, me, name):
    width = terms[0][0].shape[1]
    shapes = []
    for _, _, rows, _, tail, groups in streams:
        shapes += [jax.ShapeDtypeStruct((rows // groups + tail, width), F32)] * groups
    flat = [a for term in terms for a in term]
    out = pl.pallas_call(
        partial(spread_kernel, [len(term) for term in terms], streams),
        in_specs=[pl.BlockSpec(memory_space=pltpu.SMEM)]
        + [pl.BlockSpec(memory_space=pltpu.VMEM)] * len(flat),
        out_specs=[pl.BlockSpec(memory_space=pltpu.VMEM)] * len(shapes),
        out_shape=shapes,
        scratch_shapes=[pltpu.VMEM(term[0].shape, F32) for term in terms],
        compiler_params=params(16),
        name=name,
    )(me, *flat)
    parts = []
    for stream in streams:
        parts.append(out[: stream[-1]])
        out = out[stream[-1] :]
    return parts


def collect_kernel(places, me, *refs):
    count = sum(groups for groups, _, _ in places)
    outs = refs[count:]
    start = 0
    for i, (groups, which, at) in enumerate(places):
        piece = refs[start].shape[0]
        for m in range(groups):
            begin = pl.multiple_of(at + jnp.bitwise_xor(me[i], m) * piece, 8)
            outs[which][pl.ds(begin, piece), :] = refs[start + m][...]
        start += groups


def collect(streams, out_rows, me, name):
    flat = [a for pieces, _, _ in streams for a in pieces]
    width = flat[0].shape[1]
    return pl.pallas_call(
        partial(collect_kernel, [(len(pieces), which, at) for pieces, which, at in streams]),
        in_specs=[pl.BlockSpec(memory_space=pltpu.SMEM)]
        + [pl.BlockSpec(memory_space=pltpu.VMEM)] * len(flat),
        out_specs=[pl.BlockSpec(memory_space=pltpu.VMEM)] * len(out_rows),
        out_shape=[jax.ShapeDtypeStruct((rows, width), F32) for rows in out_rows],
        compiler_params=params(16),
        name=name,
    )(me, *flat)


def plan(body, rest):
    strata, chain = lax.axis_size("strata"), lax.axis_size("chain")
    if strata % 2 or chain % 4 or strata & (strata - 1) or chain & (chain - 1):
        return None
    across = chain // 4
    plane, line = strata // 2 * across, 4
    if body % (8 * plane * line) or rest % (8 * plane * line):
        return None
    return across, plane, line


def hop(block, strata_flip, chain_flip):
    strata, chain = lax.axis_size("strata"), lax.axis_size("chain")
    route = [
        (s * chain + c, (s ^ strata_flip) * chain + (c ^ chain_flip))
        for s in range(strata)
        for c in range(chain)
    ]
    return lax.ppermute(block, ("strata", "chain"), route)


def total_by_hops(keep, send, body, rest, groups):
    across, plane, line = groups
    strata, chain = lax.axis_index("strata"), lax.axis_index("chain")
    in_plane = strata // 2 * across + chain % across
    in_line = chain // across
    zero = jnp.int32(0)

    def plane_hops(pieces):
        return [pieces[0]] + [
            hop(pieces[m], m // across * 2, m % across) for m in range(1, plane)
        ]

    def line_hops(pieces):
        return [pieces[0]] + [hop(pieces[m], 0, m * across) for m in range(1, line)]

    end = body + rest
    tail = keep.shape[0] - end
    first_me = jnp.stack([in_plane, in_line])
    second_me = jnp.stack([in_line, in_plane])
    a, b = spread(
        [[keep, hop(send, 1, 0)]],
        [(0, 0, body, end, tail, plane), (0, body, rest, 0, 0, line)],
        first_me, "spread_first",
    )
    a, b = plane_hops(a), line_hops(b)
    body_a, body_b = body // plane, rest // line
    a, b = spread(
        [a, b],
        [(0, 0, body_a, body_a, tail, line), (1, 0, body_b, 0, 0, plane)],
        second_me, "spread_second",
    )
    a, b = line_hops(a), plane_hops(b)
    size_a, size_b = body_a // line, body_b // plane
    (a,), (note,), (b,) = spread(
        [a, b],
        [(0, 0, size_a, 0, 0, 1), (0, size_a, tail, 0, 0, 1), (1, 0, size_b, 0, 0, 1)],
        jnp.stack([zero, zero, zero]), "sums",
    )
    a, b = line_hops([a] * line), plane_hops([b] * plane)
    a, b = collect([(a, 0, 0), (b, 1, 0)], [body_a, body_b], second_me, "collect_first")
    a, b = plane_hops([a] * plane), line_hops([b] * line)
    (own,) = collect([(a, 0, 0), (b, 0, body)], [end], first_me, "collect_second")
    return own, hop(own, 1, 0), note


def finish_kernel(half, own, got, grad_in, grad_mid, grad_out):
    body, rest = grad_mid.shape[0], grad_out.shape[0] // 2

    def write(top, bottom):
        grad_mid[...] = top[0:body, :]
        grad_in[...] = bottom[0:body, :]
        grad_out[0:rest, :] = top[body:, :]
        grad_out[rest:, :] = bottom[body:, :]

    @pl.when(half[0] == 0)
    def _():
        write(own, got)

    @pl.when(half[0] != 0)
    def _():
        write(got, own)


def finish(half, own, got, shapes):
    return pl.pallas_call(
        finish_kernel,
        in_specs=[pl.BlockSpec(memory_space=pltpu.SMEM)]
        + [pl.BlockSpec(memory_space=pltpu.VMEM)] * 2,
        out_specs=[pl.BlockSpec(memory_space=pltpu.VMEM)] * 3,
        out_shape=[pltpu.HBM(shape, F32) for shape in shapes],
        compiler_params=params(16),
        name="finish",
    )(half, own, got)


def from_behind(block, axis, distance):
    devices = range(lax.axis_size(axis))
    route = [(i - distance, i) for i in devices if i - distance in devices]
    return lax.ppermute(block, axis, route)


def pipeline(cap, total_rows, half, features, events, first, entry, w_in, w_mid, w_out):
    rows = features.shape[0]
    first_row = first.reshape(1, rows)
    entry_row = entry.reshape(1, rows)
    starts = first[::TILE]
    (
        first_hidden, hidden, slope_in, slope_mid, indicator, weight, weight_top, weight_rest,
        send, note, rank,
    ) = trunk(cap, entry_row, features, events, w_in, w_mid, w_out)
    got = from_behind(send, "chain", -1)
    risk = own_risk(starts, entry, first_row, weight_top, weight_rest)
    hazard_top, hazard_rest, sums = hazards(cap, first_row, risk, indicator, got)
    got_sums = from_behind(sums, "chain", 1)
    exposure, log_part = own_exposure(starts, first, entry_row, hazard_top, hazard_rest)
    kept = (weight, indicator, hidden, slope_mid, first_hidden, slope_in)
    return backward(
        cap, total_rows ** (-0.5), half, rank, exposure, got_sums, (note, log_part), kept,
        features, w_in, w_mid, w_out,
    )


def on_device(features, events, tie_first, entry_row, w_in, w_mid, w_out):
    rows = features.shape[0]
    total_rows = rows * lax.axis_size("chain") * lax.axis_size("strata")
    block_start = lax.axis_index("chain") * rows
    first = tie_first - block_start
    entry = entry_row - block_start
    args = (features, events, first, entry, w_in, w_mid, w_out)
    shapes = (w_in.shape, w_mid.shape, w_out.shape)
    body, rest = w_mid.shape[0], w_out.shape[0] // 2
    groups = plan(body, rest)
    half = jnp.zeros((1,), I32)
    if groups:
        half = half + lax.axis_index("strata") % 2

    def run(cap):
        grad_x, keep, send = pipeline(cap, total_rows, half, *args)
        if groups:
            own, other, note = total_by_hops(keep, send, body, rest, groups)
        else:
            own, other = lax.psum((keep, send[: body + rest]), ("strata", "chain"))
            own, note = own[: body + rest], own[body + rest :]
        return note, (note[0] / total_rows, grad_x, own, other)

    def complete(kept):
        loss, grad_x, own, other = kept
        return (loss, grad_x, *finish(half, own, other, shapes))

    note, kept = run(min(GROUP, rows))
    return lax.cond(note[1, 0] > 0, lambda _: complete(run(rows)[1]), complete, kept)


def solution(mesh):
    placed = (
        P(("strata", "chain"), None),
        P(("strata", "chain"), None),
        P(("strata", "chain")),
        P(("strata", "chain")),
        P(),
        P(),
        P(),
    )
    return jax.shard_map(
        on_device,
        mesh=mesh,
        in_specs=placed,
        out_specs=(P(), P(("strata", "chain"), None), P(), P(), P()),
        check_vma=False,
    )
```

```python
from functools import partial

import jax
import jax.numpy as jnp
import numpy as np
from jax import lax
from jax.experimental import pallas as pl
from jax.experimental.pallas import tpu as pltpu
from jax.sharding import PartitionSpec as P

BITS = 15
LANES = 128
TILE = 512
DEPTH = 512
GROUP = 256
MIB = 1024 * 1024
F32 = jnp.float32
BF16 = jnp.bfloat16
I32 = jnp.int32


def two_parts(value):
    top = value.astype(BF16)
    return top, (value - top.astype(F32)).astype(BF16)


def iota(shape, dim):
    return lax.broadcasted_iota(I32, shape, dim)


def ones_where(mask):
    return jnp.where(mask, 1.0, 0.0).astype(BF16)


def dot(a, b, ca=1, cb=0):
    return lax.dot_general(a, b, (((ca,), (cb,)), ((), ())), preferred_element_type=F32)


def widen(column, width):
    return jnp.concatenate([column] * (width // column.shape[1]), axis=1)


def as_column(row):
    parts = [
        jnp.broadcast_to(row[:, k : k + LANES], (LANES, LANES)).T
        for k in range(0, row.shape[1], LANES)
    ]
    return jnp.concatenate(parts, axis=0)


def whole():
    return pl.BlockSpec(memory_space=pltpu.VMEM)


def rows_of(tile, width):
    return pl.BlockSpec((tile, width), lambda i: (i, 0))


def fixed(shape):
    return pl.BlockSpec(shape, lambda i: (0, 0), pipeline_mode=pl.Buffered(1))


def lanes_of(height, tile):
    return pl.BlockSpec((height, tile), lambda i: (0, i))


def in_hbm(array):
    return pltpu.with_memory_space_constraint(array, pltpu.HBM)


def in_vmem(array):
    return pltpu.with_memory_space_constraint(array, pltpu.VMEM)


def sent_rows(cap):
    return cap * 3 // 4 if cap == GROUP else cap


def group_rows(t, sent):
    return pl.ds(0, sent) if sent < GROUP else pl.ds(pl.multiple_of(t * GROUP, GROUP), GROUP)


def put_parts(out, chunk, value):
    rows = value.shape[0]
    at = 0 if chunk is None else pl.multiple_of(chunk * 2 * rows, 2 * rows)
    out[pl.ds(at, rows), :], out[pl.ds(at + rows, rows), :] = two_parts(value)


def twice(mask, chunk):
    parts = []
    for k in range(0, mask.shape[1], chunk):
        parts += [mask[:, k : k + chunk]] * 2
    return jnp.concatenate(parts, axis=1)


def params(mib):
    return pltpu.CompilerParams(vmem_limit_bytes=mib * MIB)


def rank_entries(entry_ref, rank_ref, note, cap):
    rows = entry_ref.shape[1]
    high = rows // LANES
    place = entry_ref[...] + rows
    crosses = place < rows
    high_hit = ones_where((iota((high, rows), 0) == (place >> 7)) & crosses)
    low_hit = jnp.where((iota((LANES, rows), 0) == (place & (LANES - 1))) & crosses, 1.0, 0.0)
    present = ones_where(dot(high_hit, low_hit.astype(BF16), 1, 1) > 0.5)
    square = (LANES, LANES)
    within = dot(present, ones_where(iota(square, 0) < iota(square, 1)))
    small = (high, high)
    ahead = dot(ones_where(iota(small, 1) < iota(small, 0)), present)
    table = within + jnp.sum(ahead, axis=1, keepdims=True)
    table_high = jnp.floor(table * (1.0 / 256.0))
    table_low = table - 256.0 * table_high
    found = 256.0 * dot(table_high.astype(BF16), high_hit, 0, 0)
    found = found + dot(table_low.astype(BF16), high_hit, 0, 0)
    rank = jnp.sum(found * low_hit, axis=0, keepdims=True)
    rank_ref[...] = jnp.where(crosses, rank.astype(I32), -1)
    count = jnp.sum(present.astype(F32))
    note[...] = jnp.where(iota(note.shape, 0) == 1, jnp.where(count > sent_rows(cap), 1.0, 0.0), 0.0)


def trunk_kernel(
    cap, entry_ref, x_ref, events_ref, byte_ref, shift_ref, w_in, w_mid, w_out,
    first_hidden, hidden, slope_in, slope_mid, indicator_out, weight, send, note,
    rank_ref,
):
    step = pl.program_id(0)
    tile = x_ref.shape[0]

    @pl.when(step == 0)
    def _():
        rank_entries(entry_ref, rank_ref, note, cap)
        send[...] = jnp.zeros_like(send)

    events = events_ref[...]
    split = jnp.concatenate([events & 255, events >> 8], axis=0).astype(F32).astype(BF16)
    spread = dot(split, byte_ref[...], 0, 0)
    bits = jnp.bitwise_and(jnp.right_shift(spread.astype(I32), shift_ref[...]), 1)
    indicator = bits.astype(F32)
    indicator_out[...] = indicator.astype(BF16)

    preact = dot(x_ref[...], w_in[...])
    sigma = jax.nn.sigmoid(preact)
    first = (preact * sigma).astype(BF16)
    first_hidden[...] = first
    slope_in[...] = sigma * (1.0 + preact * (1.0 - sigma))
    mid_pre = dot(first, w_mid[...])
    sigma = jax.nn.sigmoid(mid_pre)
    second = (mid_pre * sigma).astype(BF16)
    hidden[...] = second
    slope_mid[...] = sigma * (1.0 + mid_pre * (1.0 - sigma))
    log_hazard = dot(second, w_out[...])
    put_parts(weight, None, jnp.exp(log_hazard))
    note[0:1, :] -= jnp.sum(indicator * log_hazard, axis=0, keepdims=True)

    sent = sent_rows(cap)
    own = pl.ds(pl.multiple_of(step * tile, tile), tile)
    rank = rank_ref[:, own]
    entry = (entry_ref[:, own] + rank_ref.shape[1]).astype(F32)

    def total(t, _):
        hit = iota((GROUP, tile), 0) + t * GROUP == rank
        place = jnp.max(jnp.where(hit, entry, 0.0), axis=1, keepdims=True)
        place = jnp.broadcast_to(place, (GROUP, LANES))
        parts = [place[k : k + LANES, :].T[0:1] for k in range(0, GROUP, LANES)]
        spot = (send.shape[0] - sent, GROUP)
        place = jnp.broadcast_to(jnp.concatenate(parts, axis=1), spot)
        place = jnp.where(iota(spot, 0) == t, place, 0.0)
        send[sent:, 0:GROUP] = jnp.maximum(send[sent:, 0:GROUP], place)
        at = group_rows(t, sent)
        hit = ones_where(hit)[: min(GROUP, sent)]
        send[at, :] += dot(twice(hit, tile), weight[...])
        return 0

    lax.fori_loop(0, cap // GROUP, total, 0)


def trunk(cap, entry, features, events, w_in, w_mid, w_out):
    rows, width = features.shape
    mid = w_in.shape[1]
    wide = w_mid.shape[1]
    out_width = w_out.shape[1]
    words = events.shape[1]
    column = np.arange(out_width)
    owner = (np.arange(words)[:, None] == column // BITS).astype(np.float32)
    bit = column % BITS
    byte = jnp.asarray(np.concatenate([owner * (bit < 8), owner * (bit >= 8)]), BF16)
    shift = jnp.asarray((bit % 8)[None, :], I32)
    sent = sent_rows(cap) + -(-(cap // GROUP) // 8) * 8
    like = jax.ShapeDtypeStruct
    return pl.pallas_call(
        partial(trunk_kernel, cap),
        grid=(rows // TILE,),
        in_specs=[whole(), rows_of(TILE, width), lanes_of(words, TILE)]
        + [whole()] * 2
        + [fixed(w.shape) for w in (w_in, w_mid, w_out)],
        out_specs=[
            rows_of(TILE, mid), rows_of(TILE, wide), rows_of(TILE, mid), rows_of(TILE, wide),
            rows_of(TILE, out_width), rows_of(2 * TILE, out_width),
        ]
        + [whole()] * 3,
        out_shape=[
            pltpu.HBM((rows, mid), BF16), pltpu.HBM((rows, wide), BF16),
            pltpu.HBM((rows, mid), F32), pltpu.HBM((rows, wide), F32),
            pltpu.HBM((rows, out_width), BF16), pltpu.HBM((2 * rows, out_width), BF16),
            like((sent, out_width), F32),
            like((8, out_width), F32), like((1, rows), I32),
        ],
        compiler_params=params(28),
        name="trunk",
    )(entry, in_hbm(features), in_hbm(events.T), byte, shift, *map(in_hbm, (w_in, w_mid, w_out)))


def own_risk_kernel(starts, entry_ref, first_ref, weight, out):
    step = pl.program_id(0)
    tile = first_ref.shape[1]
    rows = weight.shape[0] // 2
    first = widen(as_column(first_ref[...]), DEPTH)
    own = pl.ds(pl.multiple_of(step * tile, tile), tile)
    out[own, :] = jnp.zeros((tile, out.shape[1]), F32)

    def part(k, _):
        at = pl.multiple_of(k * DEPTH, DEPTH)
        row = iota((tile, DEPTH), 1) + at
        entry = entry_ref[pl.ds(k, 1), :]
        mask = ones_where((row >= first) & (entry <= first))
        both = pl.ds(pl.multiple_of(k * 2 * DEPTH, 2 * DEPTH), 2 * DEPTH)
        out[own, :] += dot(twice(mask, DEPTH), weight[both, :])
        return 0

    lax.fori_loop(starts[step] // DEPTH, rows // DEPTH, part, 0)


def block_sum(flops):
    return pl.CostEstimate(flops=flops, bytes_accessed=flops // 256, transcendentals=0)


def own_risk(starts, entry, first, weight):
    rows, width = weight.shape[0] // 2, weight.shape[1]
    return pl.pallas_call(
        own_risk_kernel,
        grid=(rows // TILE,),
        in_specs=[
            pl.BlockSpec(memory_space=pltpu.SMEM), whole(), lanes_of(1, TILE),
            fixed(weight.shape),
        ],
        out_specs=whole(),
        out_shape=pltpu.VMEM((rows, width), F32),
        compiler_params=params(16),
        cost_estimate=block_sum(rows * rows * width * 4),
        name="own_risk",
    )(starts, entry.reshape(rows // DEPTH, DEPTH), first, in_hbm(weight))


def own_exposure_kernel(starts, first_ref, entry_ref, hazard, out, note):
    step = pl.program_id(0)
    tile = entry_ref.shape[1]

    @pl.when(step == 0)
    def _():
        note[...] = jnp.zeros_like(note)

    entry = widen(as_column(entry_ref[...]), DEPTH)
    row = iota((tile, DEPTH), 0) + step * tile
    own = pl.ds(pl.multiple_of(step * tile, tile), tile)
    out[own, :] = jnp.zeros((tile, out.shape[1]), F32)
    last = step * tile + tile - 1
    parts = jnp.int32(0)
    for k in range(first_ref.shape[0]):
        parts += jnp.where(starts[k * (DEPTH // TILE)] <= last, 1, 0).astype(I32)

    def part(k, _):
        first = first_ref[pl.ds(k, 1), :]
        mask = ones_where((first >= entry) & (first <= row))
        both = pl.ds(pl.multiple_of(k * 2 * DEPTH, 2 * DEPTH), 2 * DEPTH)
        out[own, :] += dot(twice(mask, DEPTH), hazard[both, :])
        return 0

    lax.fori_loop(0, parts, part, 0)
    top = hazard[pl.ds(pl.multiple_of(step * 2 * tile, tile), tile), :].astype(F32)
    rest = hazard[pl.ds(pl.multiple_of(step * 2 * tile + tile, tile), tile), :].astype(F32)
    logs = jnp.where(top > 0.0, jnp.log(top + rest), 0.0)
    note[0:1, :] -= jnp.sum(logs, axis=0, keepdims=True)


def own_exposure(starts, first, entry, hazard):
    rows, width = hazard.shape[0] // 2, hazard.shape[1]
    like = jax.ShapeDtypeStruct
    return pl.pallas_call(
        own_exposure_kernel,
        grid=(rows // TILE,),
        in_specs=[
            pl.BlockSpec(memory_space=pltpu.SMEM), whole(), lanes_of(1, TILE), whole()
        ],
        out_specs=[whole(), whole()],
        out_shape=[pltpu.VMEM((rows, width), F32), like((8, width), F32)],
        compiler_params=params(12),
        cost_estimate=block_sum(rows * rows * width * 4),
        name="own_exposure",
    )(starts, first.reshape(rows // DEPTH, DEPTH), entry, in_vmem(hazard))


def split_sum(source, parts, cap):
    sent = sent_rows(cap)
    for t in range(cap // GROUP):
        rows = min(GROUP, sent - t * GROUP)
        value = source[t * GROUP : t * GROUP + rows, :]
        if rows < GROUP:
            value = jnp.concatenate([value, jnp.zeros((GROUP - rows, value.shape[1]), F32)], axis=0)
        put_parts(parts, t, value)


def group_sum(mask, parts, t):
    at = pl.ds(pl.multiple_of(t * 2 * GROUP, 2 * GROUP), 2 * GROUP)
    return dot(twice(mask, GROUP), parts[at, :])


def hazard_kernel(
    cap, first_all, first_ref, risk, indicator_ref, got, hazard, sums, parts
):
    step = pl.program_id(0)
    tile = first_ref.shape[1]
    rows = hazard.shape[0] // 2
    own = pl.ds(pl.multiple_of(step * tile, tile), tile)

    @pl.when(step == 0)
    def _():
        split_sum(got, parts, cap)

    first = widen(as_column(first_ref[...]).astype(F32), GROUP)
    divisor = risk[own, :]
    sent = sent_rows(cap)

    def beyond(t, total):
        entry = got[pl.ds(sent + t, 1), 0:GROUP]
        return total + group_sum(ones_where(entry <= first), parts, t)

    divisor = lax.fori_loop(0, cap // GROUP, beyond, divisor)
    put_parts(hazard, step, indicator_ref[...].astype(F32) / divisor)

    @pl.when(step == pl.num_programs(0) - 1)
    def _():
        def total(t, _):
            entry = as_column(got[pl.ds(sent + t, 1), 0:GROUP])[: min(GROUP, sent)]
            entry = widen(entry, rows)
            mask = ones_where(first_all[...].astype(F32) >= entry)
            sums[group_rows(t, sent), :] = dot(twice(mask, DEPTH), hazard[...])
            return 0

        lax.fori_loop(0, cap // GROUP, total, 0)


def hazards(cap, first, risk, indicator, got):
    rows, width = risk.shape
    like = jax.ShapeDtypeStruct
    return pl.pallas_call(
        partial(hazard_kernel, cap),
        grid=(rows // TILE,),
        in_specs=[
            whole(), lanes_of(1, TILE), whole(), rows_of(TILE, width), whole()
        ],
        out_specs=[whole(), whole()],
        out_shape=[pltpu.VMEM((2 * rows, width), BF16), like((sent_rows(cap), width), F32)],
        scratch_shapes=[pltpu.VMEM((2 * cap, width), BF16)],
        compiler_params=params(20),
        name="hazards",
    )(first, first, in_vmem(risk), in_hbm(indicator), got)


def backward_kernel(
    cap, factor, half, rank_ref, exposure_ref, got, note, log_part, weight, indicator, hidden,
    slope_mid, first_hidden, slope_in, x_ref, w_in, w_mid, w_out, grad_x, keep, send,
    parts, grad_in, grad_mid, grad_out,
):
    step = pl.program_id(0)
    tile = rank_ref.shape[1]
    own = pl.ds(pl.multiple_of(step * tile, tile), tile)

    @pl.when(step == 0)
    def _():
        split_sum(got, parts, cap)
        grad_in[...] = jnp.zeros_like(grad_in)
        grad_mid[...] = jnp.zeros_like(grad_mid)
        grad_out[...] = jnp.zeros_like(grad_out)

    rank = widen(as_column(rank_ref[...]), GROUP)

    def behind(t, total):
        return total + group_sum(ones_where(rank == iota((tile, GROUP), 1) + t * GROUP), parts, t)

    exposure = lax.fori_loop(0, cap // GROUP, behind, exposure_ref[own, :])
    top = weight[pl.ds(pl.multiple_of(step * 2 * tile, tile), tile), :].astype(F32)
    rest = weight[pl.ds(pl.multiple_of(step * 2 * tile + tile, tile), tile), :].astype(F32)
    eta = ((top + rest) * exposure - indicator[own, :].astype(F32)).astype(BF16)
    grad_out[...] += dot(hidden[own, :], eta, 0, 0)
    mid = (dot(eta, w_out[...], 1, 1) * slope_mid[own, :]).astype(BF16)
    grad_mid[...] += dot(first_hidden[own, :], mid, 0, 0)
    pre = (dot(mid, w_mid[...], 1, 1) * slope_in[own, :]).astype(BF16)
    grad_in[...] += dot(x_ref[own, :], pre, 0, 0)
    grad_x[...] = dot(pre, w_in[...], 1, 1).astype(BF16)

    @pl.when(step == pl.num_programs(0) - 1)
    def _():
        body, rest = grad_mid.shape[0], grad_out.shape[0] // 2
        end = body + rest

        def write(out, block, at):
            out[0:body, :] = block[...] * factor
            out[body:end, :] = grad_out[at : at + rest, :] * factor
            out[end:, :] = note[...] + log_part[...]

        @pl.when(half[0] == 0)
        def _():
            write(keep, grad_mid, 0)
            write(send, grad_in, rest)

        @pl.when(half[0] != 0)
        def _():
            write(keep, grad_in, rest)
            write(send, grad_mid, 0)


def backward(cap, factor, half, rank, exposure, got, notes, kept, features, w_in, w_mid, w_out):
    rows, width = features.shape
    out_width = exposure.shape[1]
    halves = (w_mid.shape[0] + w_out.shape[0] // 2 + 8, out_width)
    tiles = [in_vmem(a) for a in (*kept, features)]
    weights = (w_in, w_mid, w_out)
    return pl.pallas_call(
        partial(backward_kernel, cap, factor),
        grid=(rows // TILE,),
        in_specs=[pl.BlockSpec(memory_space=pltpu.SMEM), lanes_of(1, TILE)]
        + [whole()] * (2 + len(notes))
        + [whole()] * (len(tiles) + 3),
        out_specs=[rows_of(TILE, width), whole(), whole()],
        out_shape=[
            pltpu.HBM((rows, width), BF16), pltpu.HBM(halves, F32),
            jax.ShapeDtypeStruct(halves, F32),
        ],
        scratch_shapes=[pltpu.VMEM((2 * cap, out_width), BF16)]
        + [pltpu.VMEM(w.shape, F32) for w in weights],
        compiler_params=params(20),
        name="backward",
    )(half, rank, in_vmem(exposure), got, *notes, *tiles, *weights)


def in_steps(rows, work):
    step = 16 if rows % 16 == 0 else 8
    if rows <= step:
        work(0, rows)
        return

    def body(k, _):
        work(pl.multiple_of(k * step, 8), step)
        return 0

    lax.fori_loop(0, rows // step, body, 0, unroll=2)


def spread_kernel(sizes, streams, me, *refs):
    count = sum(sizes)
    outs = iter(refs[count:])
    groups_of = []
    for size in sizes:
        groups_of.append(refs[:size])
        refs = refs[size:]

    def total(which, rows):
        value = groups_of[which][0][rows, :]
        for ref in groups_of[which][1:]:
            value = value + ref[rows, :]
        return value

    for i, (which, at, rows, tail_at, tail, groups) in enumerate(streams):
        if not groups:
            flag = jnp.max(total(which, pl.ds(at, rows)))
            next(outs)[0] = jnp.where(flag > 0.0, 1, 0).astype(I32)
            continue
        piece = rows // groups
        for m in range(groups):
            out = next(outs)
            begin = at
            if groups > 1:
                begin = pl.multiple_of(at + jnp.bitwise_xor(me[i], m) * piece, 8)

            def work(row, step, out=out, begin=begin):
                source = pl.ds(pl.multiple_of(begin + row, 8), step)
                out[pl.ds(row, step), :] = total(which, source)

            in_steps(piece, work)
            if tail:
                out[piece : piece + tail, :] = total(which, pl.ds(tail_at, tail))


def spread(terms, streams, me, name):
    width = terms[0][0].shape[1]
    shapes, places = [], []
    for _, _, rows, _, tail, groups in streams:
        if groups:
            shapes += [pltpu.VMEM((rows // groups + tail, width), F32)] * groups
            places += [pl.BlockSpec(memory_space=pltpu.VMEM)] * groups
        else:
            shapes.append(jax.ShapeDtypeStruct((1,), I32))
            places.append(pl.BlockSpec(memory_space=pltpu.SMEM))
    flat = [a for term in terms for a in term]
    out = pl.pallas_call(
        partial(spread_kernel, [len(term) for term in terms], streams),
        in_specs=[pl.BlockSpec(memory_space=pltpu.SMEM)]
        + [pl.BlockSpec(memory_space=pltpu.VMEM)] * len(flat),
        out_specs=places,
        out_shape=shapes,
        compiler_params=params(16),
        name=name,
    )(me, *flat)
    parts = []
    for stream in streams:
        parts.append(out[: max(stream[-1], 1)])
        out = out[max(stream[-1], 1) :]
    return parts


def collect_kernel(places, me, *refs):
    count = sum(groups for groups, _, _ in places)
    outs = refs[count:]
    start = 0
    for i, (groups, which, at) in enumerate(places):
        piece = refs[start].shape[0]
        for m in range(groups):
            begin = pl.multiple_of(at + jnp.bitwise_xor(me[i], m) * piece, 8)

            def work(row, step, out=outs[which], ref=refs[start + m], begin=begin):
                target = pl.ds(pl.multiple_of(begin + row, 8), step)
                out[target, :] = ref[pl.ds(row, step), :]

            in_steps(piece, work)
        start += groups


def collect(streams, out_rows, me, name):
    flat = [a for pieces, _, _ in streams for a in pieces]
    width = flat[0].shape[1]
    return pl.pallas_call(
        partial(collect_kernel, [(len(pieces), which, at) for pieces, which, at in streams]),
        in_specs=[pl.BlockSpec(memory_space=pltpu.SMEM)]
        + [pl.BlockSpec(memory_space=pltpu.VMEM)] * len(flat),
        out_specs=[pl.BlockSpec(memory_space=pltpu.VMEM)] * len(out_rows),
        out_shape=[pltpu.VMEM((rows, width), F32) for rows in out_rows],
        compiler_params=params(16),
        name=name,
    )(me, *flat)


def plan(body, rest):
    strata, chain = lax.axis_size("strata"), lax.axis_size("chain")
    if strata % 2 or chain % 4 or strata & (strata - 1) or chain & (chain - 1):
        return None
    across = chain // 4
    plane, line = strata // 2 * across, 4
    if body % (8 * plane * line) or rest % (8 * line):
        return None
    return across, plane, line


def hop(block, strata_flip, chain_flip):
    strata, chain = lax.axis_size("strata"), lax.axis_size("chain")
    route = [
        (s * chain + c, (s ^ strata_flip) * chain + (c ^ chain_flip))
        for s in range(strata)
        for c in range(chain)
    ]
    return lax.ppermute(block, ("strata", "chain"), route)


def hops(groups):
    across, plane, line = groups
    strata, chain = lax.axis_index("strata"), lax.axis_index("chain")

    def plane_hops(pieces):
        return [pieces[0]] + [
            hop(pieces[m], m // across * 2, m % across) for m in range(1, plane)
        ]

    def line_hops(pieces):
        return [pieces[0]] + [hop(pieces[m], 0, m * across) for m in range(1, line)]

    return plane_hops, line_hops, strata // 2 * across + chain % across, chain // across


def reduced(keep, send, body, rest, groups):
    plane_hops, line_hops, in_plane, in_line = hops(groups)
    _, plane, line = groups
    end = body + rest
    tail = keep.shape[0] - end
    a, b = spread(
        [[keep, hop(send, 1, 0)]],
        [(0, 0, body, end, tail, plane), (0, body, rest, 0, 0, line)],
        jnp.stack([in_plane, in_line]), "spread_first",
    )
    a, b = plane_hops(a), line_hops(b)
    size_a, size_b = body // plane, rest // line
    none = jnp.zeros((3,), I32)
    ((b,),) = spread([b], [(0, 0, size_b, 0, 0, 1)], none, "lines_summed")
    (a,) = spread(
        [a], [(0, 0, size_a, size_a, tail, line)], in_line.reshape(1), "spread_second"
    )
    a, b = line_hops(a), plane_hops([b] * plane)
    ((b,),) = spread([b], [(0, 0, size_b, 0, 0, 1)], none, "rest_summed")
    size_a = size_a // line
    (a,), (note,), (flag,) = spread(
        [a],
        [(0, 0, size_a, 0, 0, 1), (0, size_a, tail, 0, 0, 1), (0, size_a + 1, 1, 0, 0, 0)],
        none, "body_summed",
    )
    (a,) = collect(
        [(line_hops([a] * line), 0, 0)], [body // plane], in_line.reshape(1), "collect_first"
    )
    return flag, note, a, b


def gathered(a, b, body, rest, groups):
    plane_hops, line_hops, in_plane, in_line = hops(groups)
    _, plane, line = groups
    a, b = plane_hops([a] * plane), line_hops([b] * line)
    (own,) = collect(
        [(a, 0, 0), (b, 0, body)], [body + rest], jnp.stack([in_plane, in_line]), "collect_second"
    )
    return own, hop(own, 1, 0)


def place_kernel(of_core, half, block, *refs):
    grad_in, grad_mid, grad_out, sems = refs[-4:]
    body, rest = grad_mid.shape[0], grad_out.shape[0] // 2

    def write(target, at):
        copies = [
            pltpu.make_async_copy(block.at[pl.ds(0, body)], target, sems.at[0]),
            pltpu.make_async_copy(
                block.at[pl.ds(body, rest)], grad_out.at[pl.ds(at, rest)], sems.at[1]
            ),
        ]
        for copy in copies:
            copy.start()
        for copy in copies:
            copy.wait()

    @pl.when(half[0] == of_core)
    def _():
        write(grad_mid, 0)

    @pl.when(half[0] != of_core)
    def _():
        write(grad_in, rest)


def place(of_core, half, block, shapes, results):
    somewhere = pl.BlockSpec(memory_space=pl.ANY)
    return pl.pallas_call(
        partial(place_kernel, of_core),
        in_specs=[
            pl.BlockSpec(memory_space=pltpu.SMEM), pl.BlockSpec(memory_space=pltpu.VMEM)
        ]
        + [somewhere] * len(results),
        out_specs=[somewhere] * 3,
        out_shape=[pltpu.HBM(shape, F32) for shape in shapes],
        scratch_shapes=[pltpu.SemaphoreType.DMA((2,))],
        input_output_aliases={2 + i: i for i in range(len(results))},
        compiler_params=params(16),
        name="place",
    )(half, block, *results)


def finish(half, own, got, shapes):
    results = place(0, half, own, shapes, ())
    return place(1, half, got, shapes, results)


def from_behind(block, axis, distance):
    devices = range(lax.axis_size(axis))
    route = [(i - distance, i) for i in devices if i - distance in devices]
    return lax.ppermute(block, axis, route)


def pipeline(cap, total_rows, half, features, events, first, entry, w_in, w_mid, w_out):
    rows = features.shape[0]
    first_row = first.reshape(1, rows)
    entry_row = entry.reshape(1, rows)
    starts = first[::TILE]
    (
        first_hidden, hidden, slope_in, slope_mid, indicator, weight, send, note, rank,
    ) = trunk(cap, entry_row, features, events, w_in, w_mid, w_out)
    got = from_behind(send, "chain", -1)
    risk = own_risk(starts, entry, first_row, weight)
    hazard, sums = hazards(cap, first_row, risk, indicator, got)
    got_sums = from_behind(sums, "chain", 1)
    exposure, log_part = own_exposure(starts, first, entry_row, hazard)
    kept = (weight, indicator, hidden, slope_mid, first_hidden, slope_in)
    return backward(
        cap, total_rows ** (-0.5), half, rank, exposure, got_sums, (note, log_part), kept,
        features, w_in, w_mid, w_out,
    )


def on_device(features, events, tie_first, entry_row, w_in, w_mid, w_out):
    rows = features.shape[0]
    total_rows = rows * lax.axis_size("chain") * lax.axis_size("strata")
    block_start = lax.axis_index("chain") * rows
    first = tie_first - block_start
    entry = entry_row - block_start
    args = (features, events, first, entry, w_in, w_mid, w_out)
    shapes = (w_in.shape, w_mid.shape, w_out.shape)
    body, rest = w_mid.shape[0], w_out.shape[0] // 2
    end = body + rest
    groups = plan(body, rest)
    half = jnp.zeros((1,), I32)
    if groups:
        half = half + lax.axis_index("strata") % 2

    def run(cap):
        grad_x, keep, send = pipeline(cap, total_rows, half, *args)
        if groups:
            flag, note, a, b = reduced(keep, send, body, rest, groups)
        else:
            a, b = lax.psum((keep, send[:end]), ("strata", "chain"))
            a, note = a[:end], a[end:]
            flag = (note[1, 0:1] > 0).astype(I32)
        return flag, note, grad_x, a, b

    _, note, grad_x, a, b = lax.while_loop(
        lambda state: state[0][0] > 0, lambda _: run(rows), run(min(GROUP, rows))
    )
    own, other = gathered(a, b, body, rest, groups) if groups else (a, b)
    return (note[0] / total_rows, grad_x, *finish(half, own, other, shapes))


def solution(mesh):
    placed = (
        P(("strata", "chain"), None),
        P(("strata", "chain"), None),
        P(("strata", "chain")),
        P(("strata", "chain")),
        P(),
        P(),
        P(),
    )
    return jax.shard_map(
        on_device,
        mesh=mesh,
        in_specs=placed,
        out_specs=(P(), P(("strata", "chain"), None), P(), P(), P()),
        check_vma=False,
    )
```

```python
from functools import partial

import jax
import jax.numpy as jnp
import numpy as np
from jax import lax
from jax.experimental import pallas as pl
from jax.experimental.pallas import tpu as pltpu
from jax.sharding import PartitionSpec as P

BITS = 15
LANES = 128
TILE = 512
DEPTH = 512
GROUP = 256
MIB = 1024 * 1024
F32 = jnp.float32
BF16 = jnp.bfloat16
I32 = jnp.int32


def two_parts(value):
    top = value.astype(BF16)
    return top, (value - top.astype(F32)).astype(BF16)


def iota(shape, dim):
    return lax.broadcasted_iota(I32, shape, dim)


def ones_where(mask):
    return jnp.where(mask, 1.0, 0.0).astype(BF16)


def dot(a, b, ca=1, cb=0):
    return lax.dot_general(a, b, (((ca,), (cb,)), ((), ())), preferred_element_type=F32)


def widen(column, width):
    return jnp.concatenate([column] * (width // column.shape[1]), axis=1)


def as_column(row):
    parts = [
        jnp.broadcast_to(row[:, k : k + LANES], (LANES, LANES)).T
        for k in range(0, row.shape[1], LANES)
    ]
    return jnp.concatenate(parts, axis=0)


def whole():
    return pl.BlockSpec(memory_space=pltpu.VMEM)


def rows_of(tile, width):
    return pl.BlockSpec((tile, width), lambda i: (i, 0))


def fixed(shape):
    return pl.BlockSpec(shape, lambda i: (0, 0), pipeline_mode=pl.Buffered(1))


def lanes_of(height, tile):
    return pl.BlockSpec((height, tile), lambda i: (0, i))


def in_hbm(array):
    return pltpu.with_memory_space_constraint(array, pltpu.HBM)


def in_vmem(array):
    return pltpu.with_memory_space_constraint(array, pltpu.VMEM)


def sent_rows(cap):
    return cap * 3 // 4 if cap == GROUP else cap


def group_rows(t, sent):
    return pl.ds(0, sent) if sent < GROUP else pl.ds(pl.multiple_of(t * GROUP, GROUP), GROUP)


def put_parts(out, chunk, value):
    rows = value.shape[0]
    at = 0 if chunk is None else pl.multiple_of(chunk * 2 * rows, 2 * rows)
    out[pl.ds(at, rows), :], out[pl.ds(at + rows, rows), :] = two_parts(value)


def twice(mask, chunk):
    parts = []
    for k in range(0, mask.shape[1], chunk):
        parts += [mask[:, k : k + chunk]] * 2
    return jnp.concatenate(parts, axis=1)


def params(mib):
    return pltpu.CompilerParams(vmem_limit_bytes=mib * MIB)


def rank_entries(entry, rank_ref, note, cap):
    rows = entry.shape[1]
    high = rows // LANES
    place = entry + rows
    crosses = place < rows
    high_hit = ones_where((iota((high, rows), 0) == (place >> 7)) & crosses)
    low_hit = jnp.where((iota((LANES, rows), 0) == (place & (LANES - 1))) & crosses, 1.0, 0.0)
    present = ones_where(dot(high_hit, low_hit.astype(BF16), 1, 1) > 0.5)
    square = (LANES, LANES)
    within = dot(present, ones_where(iota(square, 0) < iota(square, 1)))
    small = (high, high)
    ahead = dot(ones_where(iota(small, 1) < iota(small, 0)), present)
    table = within + jnp.sum(ahead, axis=1, keepdims=True)
    table_high = jnp.floor(table * (1.0 / 256.0))
    table_low = table - 256.0 * table_high
    found = 256.0 * dot(table_high.astype(BF16), high_hit, 0, 0)
    found = found + dot(table_low.astype(BF16), high_hit, 0, 0)
    rank = jnp.sum(found * low_hit, axis=0, keepdims=True)
    rank_ref[...] = jnp.where(crosses, rank.astype(I32), -1)
    count = jnp.sum(present.astype(F32))
    note[...] = jnp.where(iota(note.shape, 0) == 1, jnp.where(count > sent_rows(cap), 1.0, 0.0), 0.0)


def trunk_kernel(
    cap, block_start, entry_ref, x_ref, events_ref, byte_ref, shift_ref, w_in, w_mid, w_out,
    first_hidden, hidden, slope_in, slope_mid, indicator_out, weight, send, note,
    rank_ref,
):
    step = pl.program_id(0)
    tile = x_ref.shape[0]

    @pl.when(step == 0)
    def _():
        rank_entries(entry_ref[...] - block_start[0], rank_ref, note, cap)
        send[...] = jnp.zeros_like(send)

    events = events_ref[...]
    split = jnp.concatenate([events & 255, events >> 8], axis=0).astype(F32).astype(BF16)
    spread = dot(split, byte_ref[...], 0, 0)
    bits = jnp.bitwise_and(jnp.right_shift(spread.astype(I32), shift_ref[...]), 1)
    indicator = bits.astype(F32)
    indicator_out[...] = indicator.astype(BF16)

    preact = dot(x_ref[...], w_in[...])
    sigma = jax.nn.sigmoid(preact)
    first = (preact * sigma).astype(BF16)
    first_hidden[...] = first
    slope_in[...] = sigma * (1.0 + preact * (1.0 - sigma))
    mid_pre = dot(first, w_mid[...])
    sigma = jax.nn.sigmoid(mid_pre)
    second = (mid_pre * sigma).astype(BF16)
    hidden[...] = second
    slope_mid[...] = sigma * (1.0 + mid_pre * (1.0 - sigma))
    log_hazard = dot(second, w_out[...])
    put_parts(weight, None, jnp.exp(log_hazard))
    note[0:1, :] -= jnp.sum(indicator * log_hazard, axis=0, keepdims=True)

    sent = sent_rows(cap)
    own = pl.ds(pl.multiple_of(step * tile, tile), tile)
    rank = rank_ref[:, own]
    entry = (entry_ref[:, own] - block_start[0] + rank_ref.shape[1]).astype(F32)

    def total(t, _):
        hit = iota((GROUP, tile), 0) + t * GROUP == rank
        place = jnp.max(jnp.where(hit, entry, 0.0), axis=1, keepdims=True)
        place = jnp.broadcast_to(place, (GROUP, LANES))
        parts = [place[k : k + LANES, :].T[0:1] for k in range(0, GROUP, LANES)]
        spot = (send.shape[0] - sent, GROUP)
        place = jnp.broadcast_to(jnp.concatenate(parts, axis=1), spot)
        place = jnp.where(iota(spot, 0) == t, place, 0.0)
        send[sent:, 0:GROUP] = jnp.maximum(send[sent:, 0:GROUP], place)
        at = group_rows(t, sent)
        hit = ones_where(hit)[: min(GROUP, sent)]
        send[at, :] += dot(twice(hit, tile), weight[...])
        return 0

    lax.fori_loop(0, cap // GROUP, total, 0)


def trunk(cap, block_start, entry, features, events, w_in, w_mid, w_out):
    rows, width = features.shape
    mid = w_in.shape[1]
    wide = w_mid.shape[1]
    out_width = w_out.shape[1]
    words = events.shape[1]
    column = np.arange(out_width)
    owner = (np.arange(words)[:, None] == column // BITS).astype(np.float32)
    bit = column % BITS
    byte = jnp.asarray(np.concatenate([owner * (bit < 8), owner * (bit >= 8)]), BF16)
    shift = jnp.asarray((bit % 8)[None, :], I32)
    sent = sent_rows(cap) + -(-(cap // GROUP) // 8) * 8
    constant = (byte, shift, w_in, w_mid, w_out)
    like = jax.ShapeDtypeStruct
    return pl.pallas_call(
        partial(trunk_kernel, cap),
        grid=(rows // TILE,),
        in_specs=[
            pl.BlockSpec(memory_space=pltpu.SMEM), fixed((1, rows)), rows_of(TILE, width),
            lanes_of(words, TILE),
        ]
        + [fixed(a.shape) for a in constant],
        out_specs=[
            rows_of(TILE, mid), rows_of(TILE, wide), rows_of(TILE, mid), rows_of(TILE, wide),
            rows_of(TILE, out_width), rows_of(2 * TILE, out_width),
        ]
        + [whole()] * 3,
        out_shape=[
            pltpu.HBM((rows, mid), BF16), pltpu.HBM((rows, wide), BF16),
            pltpu.HBM((rows, mid), F32), pltpu.HBM((rows, wide), F32),
            pltpu.HBM((rows, out_width), BF16), pltpu.HBM((2 * rows, out_width), BF16),
            like((sent, out_width), F32),
            like((8, out_width), F32), like((1, rows), I32),
        ],
        compiler_params=params(28),
        name="trunk",
    )(block_start, *map(in_hbm, (entry, features, events.T, *constant)))


def own_risk_kernel(starts, entry_ref, first_ref, weight, out):
    step = pl.program_id(0)
    tile = first_ref.shape[1]
    rows = weight.shape[0] // 2
    first = widen(as_column(first_ref[...]), DEPTH)
    own = pl.ds(pl.multiple_of(step * tile, tile), tile)
    out[own, :] = jnp.zeros((tile, out.shape[1]), F32)

    def part(k, _):
        at = pl.multiple_of(k * DEPTH, DEPTH)
        row = iota((tile, DEPTH), 1) + at
        entry = entry_ref[pl.ds(k, 1), :]
        mask = ones_where((row >= first) & (entry <= first))
        both = pl.ds(pl.multiple_of(k * 2 * DEPTH, 2 * DEPTH), 2 * DEPTH)
        out[own, :] += dot(twice(mask, DEPTH), weight[both, :])
        return 0

    lax.fori_loop(starts[step] // DEPTH, rows // DEPTH, part, 0)


def block_sum(flops):
    return pl.CostEstimate(flops=flops, bytes_accessed=flops // 256, transcendentals=0)


def own_risk(starts, entry, first, weight):
    rows, width = weight.shape[0] // 2, weight.shape[1]
    return pl.pallas_call(
        own_risk_kernel,
        grid=(rows // TILE,),
        in_specs=[
            pl.BlockSpec(memory_space=pltpu.SMEM), whole(), lanes_of(1, TILE),
            fixed(weight.shape),
        ],
        out_specs=whole(),
        out_shape=pltpu.VMEM((rows, width), F32),
        compiler_params=params(16),
        cost_estimate=block_sum(rows * rows * width * 4),
        name="own_risk",
    )(starts, entry.reshape(rows // DEPTH, DEPTH), first, in_hbm(weight))


def own_exposure_kernel(starts, first_ref, entry_ref, hazard, out, note):
    step = pl.program_id(0)
    tile = entry_ref.shape[1]

    @pl.when(step == 0)
    def _():
        note[...] = jnp.zeros_like(note)

    entry = widen(as_column(entry_ref[...]), DEPTH)
    row = iota((tile, DEPTH), 0) + step * tile
    own = pl.ds(pl.multiple_of(step * tile, tile), tile)
    last = step * tile + tile - 1
    parts = jnp.int32(0)
    for k in range(first_ref.shape[0]):
        parts += jnp.where(starts[k * (DEPTH // TILE)] <= last, 1, 0).astype(I32)

    def part(k):
        first = first_ref[pl.ds(k, 1), :]
        mask = ones_where((first >= entry) & (first <= row))
        both = pl.ds(pl.multiple_of(k * 2 * DEPTH, 2 * DEPTH), 2 * DEPTH)
        return dot(twice(mask, DEPTH), hazard[both, :])

    def others(i, _):
        out[own, :] += part(i + jnp.where(i >= step, 1, 0).astype(I32))
        return 0

    out[own, :] = part(step)
    top = hazard[pl.ds(pl.multiple_of(step * 2 * tile, tile), tile), :].astype(F32)
    rest = hazard[pl.ds(pl.multiple_of(step * 2 * tile + tile, tile), tile), :].astype(F32)
    logs = jnp.where(top > 0.0, jnp.log(top + rest), 0.0)
    note[0:1, :] -= jnp.sum(logs, axis=0, keepdims=True)
    lax.fori_loop(0, parts - 1, others, 0)


def own_exposure(starts, first, entry, hazard):
    rows, width = hazard.shape[0] // 2, hazard.shape[1]
    like = jax.ShapeDtypeStruct
    return pl.pallas_call(
        own_exposure_kernel,
        grid=(rows // TILE,),
        in_specs=[
            pl.BlockSpec(memory_space=pltpu.SMEM), whole(), lanes_of(1, TILE), whole()
        ],
        out_specs=[whole(), whole()],
        out_shape=[pltpu.VMEM((rows, width), F32), like((8, width), F32)],
        compiler_params=params(12),
        cost_estimate=block_sum(rows * rows * width * 4),
        name="own_exposure",
    )(starts, first.reshape(rows // DEPTH, DEPTH), entry, in_vmem(hazard))


def split_sum(source, parts, cap):
    sent = sent_rows(cap)
    for t in range(cap // GROUP):
        rows = min(GROUP, sent - t * GROUP)
        value = source[t * GROUP : t * GROUP + rows, :]
        if rows < GROUP:
            value = jnp.concatenate([value, jnp.zeros((GROUP - rows, value.shape[1]), F32)], axis=0)
        put_parts(parts, t, value)


def group_sum(mask, parts, t):
    at = pl.ds(pl.multiple_of(t * 2 * GROUP, 2 * GROUP), 2 * GROUP)
    return dot(twice(mask, GROUP), parts[at, :])


def hazard_kernel(
    cap, first_all, first_ref, risk, indicator_ref, got, hazard, sums, parts
):
    step = pl.program_id(0)
    tile = first_ref.shape[1]
    rows = hazard.shape[0] // 2
    own = pl.ds(pl.multiple_of(step * tile, tile), tile)

    @pl.when(step == 0)
    def _():
        split_sum(got, parts, cap)

    first = widen(as_column(first_ref[...]).astype(F32), GROUP)
    divisor = risk[own, :]
    sent = sent_rows(cap)

    def beyond(t, total):
        entry = got[pl.ds(sent + t, 1), 0:GROUP]
        return total + group_sum(ones_where(entry <= first), parts, t)

    divisor = lax.fori_loop(0, cap // GROUP, beyond, divisor)
    put_parts(hazard, step, indicator_ref[...].astype(F32) / divisor)

    @pl.when(step == pl.num_programs(0) - 1)
    def _():
        def total(t, _):
            entry = as_column(got[pl.ds(sent + t, 1), 0:GROUP])[: min(GROUP, sent)]
            entry = widen(entry, rows)
            mask = ones_where(first_all[...].astype(F32) >= entry)
            sums[group_rows(t, sent), :] = dot(twice(mask, DEPTH), hazard[...])
            return 0

        lax.fori_loop(0, cap // GROUP, total, 0)


def hazards(cap, first, risk, indicator, got):
    rows, width = risk.shape
    like = jax.ShapeDtypeStruct
    return pl.pallas_call(
        partial(hazard_kernel, cap),
        grid=(rows // TILE,),
        in_specs=[
            whole(), lanes_of(1, TILE), whole(), rows_of(TILE, width), whole()
        ],
        out_specs=[whole(), whole()],
        out_shape=[pltpu.VMEM((2 * rows, width), BF16), like((sent_rows(cap), width), F32)],
        scratch_shapes=[pltpu.VMEM((2 * cap, width), BF16)],
        compiler_params=params(20),
        name="hazards",
    )(first, first, in_vmem(risk), in_hbm(indicator), got)


def backward_kernel(
    cap, factor, half, rank_ref, exposure_ref, got, note, log_part, weight, indicator, hidden,
    slope_mid, first_hidden, slope_in, x_ref, w_in, w_mid, w_out, grad_x, keep, send,
    parts, grad_in, grad_mid, grad_out,
):
    step = pl.program_id(0)
    tile = rank_ref.shape[1]
    own = pl.ds(pl.multiple_of(step * tile, tile), tile)

    @pl.when(step == 0)
    def _():
        split_sum(got, parts, cap)
        grad_in[...] = jnp.zeros_like(grad_in)
        grad_mid[...] = jnp.zeros_like(grad_mid)
        grad_out[...] = jnp.zeros_like(grad_out)

    rank = widen(as_column(rank_ref[...]), GROUP)

    def behind(t, total):
        return total + group_sum(ones_where(rank == iota((tile, GROUP), 1) + t * GROUP), parts, t)

    exposure = lax.fori_loop(0, cap // GROUP, behind, exposure_ref[own, :])
    top = weight[pl.ds(pl.multiple_of(step * 2 * tile, tile), tile), :].astype(F32)
    rest = weight[pl.ds(pl.multiple_of(step * 2 * tile + tile, tile), tile), :].astype(F32)
    eta = ((top + rest) * exposure - indicator[own, :].astype(F32)).astype(BF16)
    grad_out[...] += dot(hidden[own, :], eta, 0, 0)
    mid = (dot(eta, w_out[...], 1, 1) * slope_mid[own, :]).astype(BF16)
    grad_mid[...] += dot(first_hidden[own, :], mid, 0, 0)
    pre = (dot(mid, w_mid[...], 1, 1) * slope_in[own, :]).astype(BF16)
    grad_in[...] += dot(x_ref[own, :], pre, 0, 0)
    grad_x[...] = dot(pre, w_in[...], 1, 1).astype(BF16)

    @pl.when(step == pl.num_programs(0) - 1)
    def _():
        body, rest = grad_mid.shape[0], grad_out.shape[0] // 2
        end = body + rest

        def write(out, block, at):
            out[0:body, :] = block[...] * factor
            out[body:end, :] = grad_out[at : at + rest, :] * factor
            out[end:, :] = note[...] + log_part[...]

        @pl.when(half[0] == 0)
        def _():
            write(keep, grad_mid, 0)
            write(send, grad_in, rest)

        @pl.when(half[0] != 0)
        def _():
            write(keep, grad_in, rest)
            write(send, grad_mid, 0)


def backward(cap, factor, half, rank, exposure, got, notes, kept, features, w_in, w_mid, w_out):
    rows, width = features.shape
    out_width = exposure.shape[1]
    halves = (w_mid.shape[0] + w_out.shape[0] // 2 + 8, out_width)
    tiles = [in_vmem(a) for a in (*kept, features)]
    weights = (w_in, w_mid, w_out)
    return pl.pallas_call(
        partial(backward_kernel, cap, factor),
        grid=(rows // TILE,),
        in_specs=[pl.BlockSpec(memory_space=pltpu.SMEM), lanes_of(1, TILE)]
        + [whole()] * (2 + len(notes))
        + [whole()] * (len(tiles) + 3),
        out_specs=[rows_of(TILE, width), whole(), whole()],
        out_shape=[
            pltpu.HBM((rows, width), BF16), pltpu.HBM(halves, F32),
            jax.ShapeDtypeStruct(halves, F32),
        ],
        scratch_shapes=[pltpu.VMEM((2 * cap, out_width), BF16)]
        + [pltpu.VMEM(w.shape, F32) for w in weights],
        compiler_params=params(20),
        name="backward",
    )(half, rank, in_vmem(exposure), got, *notes, *tiles, *weights)


def in_steps(rows, work):
    step = 16 if rows % 16 == 0 else 8
    if rows <= step:
        work(0, rows)
        return

    def body(k, _):
        work(pl.multiple_of(k * step, 8), step)
        return 0

    lax.fori_loop(0, rows // step, body, 0, unroll=2)


def spread_kernel(sizes, streams, fetch, me, *refs):
    count = sum(sizes)
    outs = iter(refs[count:])
    if fetch:
        held, sems = refs[-1 - count : -1], refs[-1]
        copies = [
            pltpu.make_async_copy(refs[i], held[i], sems.at[i]) for i in range(count)
        ]
        for copy in copies:
            copy.start()
        for copy in copies:
            copy.wait()
        refs = held
    groups_of = []
    for size in sizes:
        groups_of.append(refs[:size])
        refs = refs[size:]

    def total(which, rows):
        value = groups_of[which][0][rows, :]
        for ref in groups_of[which][1:]:
            value = value + ref[rows, :]
        return value

    for i, (which, at, rows, tail_at, tail, groups) in enumerate(streams):
        if not groups:
            flag = jnp.max(total(which, pl.ds(at, rows)))
            next(outs)[0] = jnp.where(flag > 0.0, 1, 0).astype(I32)
            continue
        piece = rows // groups
        for m in range(groups):
            out = next(outs)
            begin = at
            if groups > 1:
                begin = pl.multiple_of(at + jnp.bitwise_xor(me[i], m) * piece, 8)

            def work(row, step, out=out, begin=begin):
                source = pl.ds(pl.multiple_of(begin + row, 8), step)
                out[pl.ds(row, step), :] = total(which, source)

            in_steps(piece, work)
            if tail:
                out[piece : piece + tail, :] = total(which, pl.ds(tail_at, tail))


def spread(terms, streams, me, name, fetch=False):
    width = terms[0][0].shape[1]
    shapes, places = [], []
    for _, _, rows, _, tail, groups in streams:
        if groups:
            shapes += [pltpu.VMEM((rows // groups + tail, width), F32)] * groups
            places += [pl.BlockSpec(memory_space=pltpu.VMEM)] * groups
        else:
            shapes.append(jax.ShapeDtypeStruct((1,), I32))
            places.append(pl.BlockSpec(memory_space=pltpu.SMEM))
    flat = [a for term in terms for a in term]
    scratch = [pltpu.VMEM(a.shape, F32) for a in flat] + [pltpu.SemaphoreType.DMA((len(flat),))]
    out = pl.pallas_call(
        partial(spread_kernel, [len(term) for term in terms], streams, fetch),
        in_specs=[pl.BlockSpec(memory_space=pltpu.SMEM)]
        + [pl.BlockSpec(memory_space=pl.ANY if fetch else pltpu.VMEM)] * len(flat),
        out_specs=places,
        out_shape=shapes,
        scratch_shapes=scratch if fetch else [],
        compiler_params=params(16),
        name=name,
    )(me, *flat)
    parts = []
    for stream in streams:
        parts.append(out[: max(stream[-1], 1)])
        out = out[max(stream[-1], 1) :]
    return parts


def collect_kernel(places, me, *refs):
    count = sum(groups for groups, _, _ in places)
    outs = refs[count:]
    start = 0
    for i, (groups, which, at) in enumerate(places):
        piece = refs[start].shape[0]
        for m in range(groups):
            begin = pl.multiple_of(at + jnp.bitwise_xor(me[i], m) * piece, 8)

            def work(row, step, out=outs[which], ref=refs[start + m], begin=begin):
                target = pl.ds(pl.multiple_of(begin + row, 8), step)
                out[target, :] = ref[pl.ds(row, step), :]

            in_steps(piece, work)
        start += groups


def collect(streams, out_rows, me, name):
    flat = [a for pieces, _, _ in streams for a in pieces]
    width = flat[0].shape[1]
    return pl.pallas_call(
        partial(collect_kernel, [(len(pieces), which, at) for pieces, which, at in streams]),
        in_specs=[pl.BlockSpec(memory_space=pltpu.SMEM)]
        + [pl.BlockSpec(memory_space=pltpu.VMEM)] * len(flat),
        out_specs=[pl.BlockSpec(memory_space=pltpu.VMEM)] * len(out_rows),
        out_shape=[pltpu.VMEM((rows, width), F32) for rows in out_rows],
        compiler_params=params(16),
        name=name,
    )(me, *flat)


def plan(body, rest):
    strata, chain = lax.axis_size("strata"), lax.axis_size("chain")
    if strata % 2 or chain % 4 or strata & (strata - 1) or chain & (chain - 1):
        return None
    across = chain // 4
    plane, line = strata // 2 * across, 4
    if body % (8 * plane * line) or rest % (8 * line):
        return None
    return across, plane, line


def hop(block, strata_flip, chain_flip):
    strata, chain = lax.axis_size("strata"), lax.axis_size("chain")
    route = [
        (s * chain + c, (s ^ strata_flip) * chain + (c ^ chain_flip))
        for s in range(strata)
        for c in range(chain)
    ]
    return lax.ppermute(block, ("strata", "chain"), route)


def hops(groups):
    across, plane, line = groups
    strata, chain = lax.axis_index("strata"), lax.axis_index("chain")

    def plane_hops(pieces):
        return [pieces[0]] + [
            hop(pieces[m], m // across * 2, m % across) for m in range(1, plane)
        ]

    def line_hops(pieces):
        return [pieces[0]] + [hop(pieces[m], 0, m * across) for m in range(1, line)]

    return plane_hops, line_hops, strata // 2 * across + chain % across, chain // across


def reduced(keep, send, body, rest, groups):
    plane_hops, line_hops, in_plane, in_line = hops(groups)
    _, plane, line = groups
    end = body + rest
    tail = keep.shape[0] - end
    a, b = spread(
        [[in_hbm(keep), hop(send, 1, 0)]],
        [(0, 0, body, end, tail, plane), (0, body, rest, 0, 0, line)],
        jnp.stack([in_plane, in_line]), "spread_first", fetch=True,
    )
    a, b = plane_hops(a), line_hops(b)
    size_a, size_b = body // plane, rest // line
    none = jnp.zeros((3,), I32)
    ((b,),) = spread([b], [(0, 0, size_b, 0, 0, 1)], none, "lines_summed")
    (a,) = spread(
        [a], [(0, 0, size_a, size_a, tail, line)], in_line.reshape(1), "spread_second"
    )
    a, b = line_hops(a), plane_hops([b] * plane)
    ((b,),) = spread([b], [(0, 0, size_b, 0, 0, 1)], none, "rest_summed")
    size_a = size_a // line
    (a,), (note,), (flag,) = spread(
        [a],
        [(0, 0, size_a, 0, 0, 1), (0, size_a, tail, 0, 0, 1), (0, size_a + 1, 1, 0, 0, 0)],
        none, "body_summed",
    )
    (a,) = collect(
        [(line_hops([a] * line), 0, 0)], [body // plane], in_line.reshape(1), "collect_first"
    )
    return flag, note, a, b


def gathered(a, b, body, rest, groups):
    plane_hops, line_hops, in_plane, in_line = hops(groups)
    _, plane, line = groups
    a, b = plane_hops([a] * plane), line_hops([b] * line)
    (own,) = collect(
        [(a, 0, 0), (b, 0, body)], [body + rest], jnp.stack([in_plane, in_line]), "collect_second"
    )
    return own, hop(own, 1, 0)


def place_kernel(of_core, half, block, *refs):
    grad_in, grad_mid, grad_out, sems = refs[-4:]
    body, rest = grad_mid.shape[0], grad_out.shape[0] // 2

    def write(target, at):
        copies = [
            pltpu.make_async_copy(block.at[pl.ds(0, body)], target, sems.at[0]),
            pltpu.make_async_copy(
                block.at[pl.ds(body, rest)], grad_out.at[pl.ds(at, rest)], sems.at[1]
            ),
        ]
        for copy in copies:
            copy.start()
        for copy in copies:
            copy.wait()

    @pl.when(half[0] == of_core)
    def _():
        write(grad_mid, 0)

    @pl.when(half[0] != of_core)
    def _():
        write(grad_in, rest)


def place(of_core, half, block, shapes, results):
    somewhere = pl.BlockSpec(memory_space=pl.ANY)
    return pl.pallas_call(
        partial(place_kernel, of_core),
        in_specs=[
            pl.BlockSpec(memory_space=pltpu.SMEM), pl.BlockSpec(memory_space=pltpu.VMEM)
        ]
        + [somewhere] * len(results),
        out_specs=[somewhere] * 3,
        out_shape=[pltpu.HBM(shape, F32) for shape in shapes],
        scratch_shapes=[pltpu.SemaphoreType.DMA((2,))],
        input_output_aliases={2 + i: i for i in range(len(results))},
        compiler_params=params(16),
        name="place",
    )(half, block, *results)


def finish(half, own, got, shapes):
    results = place(0, half, own, shapes, ())
    return place(1, half, got, shapes, results)


def from_behind(block, axis, distance):
    devices = range(lax.axis_size(axis))
    route = [(i - distance, i) for i in devices if i - distance in devices]
    return lax.ppermute(block, axis, route)


def pipeline(cap, total_rows, half, features, events, tie_first, entry_row, w_in, w_mid, w_out):
    rows = features.shape[0]
    block_start = (lax.axis_index("chain") * rows).reshape(1)
    first = tie_first - block_start
    entry = entry_row - block_start
    first_line = first.reshape(1, rows)
    entry_line = entry.reshape(1, rows)
    starts = first[::TILE]
    (
        first_hidden, hidden, slope_in, slope_mid, indicator, weight, send, note, rank,
    ) = trunk(
        cap, block_start, entry_row.reshape(1, rows), features, events, w_in, w_mid, w_out
    )
    got = from_behind(send, "chain", -1)
    risk = own_risk(starts, entry, first_line, weight)
    hazard, sums = hazards(cap, first_line, risk, indicator, got)
    got_sums = from_behind(sums, "chain", 1)
    exposure, log_part = own_exposure(starts, first, entry_line, hazard)
    kept = (weight, indicator, hidden, slope_mid, first_hidden, slope_in)
    return backward(
        cap, total_rows ** (-0.5), half, rank, exposure, got_sums, (note, log_part), kept,
        features, w_in, w_mid, w_out,
    )


def on_device(features, events, tie_first, entry_row, w_in, w_mid, w_out):
    rows = features.shape[0]
    total_rows = rows * lax.axis_size("chain") * lax.axis_size("strata")
    args = (features, events, tie_first, entry_row, w_in, w_mid, w_out)
    shapes = (w_in.shape, w_mid.shape, w_out.shape)
    body, rest = w_mid.shape[0], w_out.shape[0] // 2
    end = body + rest
    groups = plan(body, rest)
    half = jnp.zeros((1,), I32)
    if groups:
        half = half + lax.axis_index("strata") % 2

    def run(cap):
        grad_x, keep, send = pipeline(cap, total_rows, half, *args)
        if groups:
            flag, note, a, b = reduced(keep, send, body, rest, groups)
        else:
            a, b = lax.psum((keep, send[:end]), ("strata", "chain"))
            a, note = a[:end], a[end:]
            flag = (note[1, 0:1] > 0).astype(I32)
        return flag, note, grad_x, a, b

    _, note, grad_x, a, b = lax.while_loop(
        lambda state: state[0][0] > 0, lambda _: run(rows), run(min(GROUP, rows))
    )
    own, other = gathered(a, b, body, rest, groups) if groups else (a, b)
    return (note[0] / total_rows, grad_x, *finish(half, own, other, shapes))


def solution(mesh):
    placed = (
        P(("strata", "chain"), None),
        P(("strata", "chain"), None),
        P(("strata", "chain")),
        P(("strata", "chain")),
        P(),
        P(),
        P(),
    )
    return jax.shard_map(
        on_device,
        mesh=mesh,
        in_specs=placed,
        out_specs=(P(), P(("strata", "chain"), None), P(), P(), P()),
        check_vma=False,
    )
```

```python
from functools import partial

import jax
import jax.numpy as jnp
import numpy as np
from jax import lax
from jax.experimental import pallas as pl
from jax.experimental.pallas import tpu as pltpu
from jax.sharding import PartitionSpec as P

BITS = 15
LANES = 128
TILE = 512
DEPTH = 512
GROUP = 256
MIB = 1024 * 1024
F32 = jnp.float32
BF16 = jnp.bfloat16
I32 = jnp.int32


def two_parts(value):
    top = value.astype(BF16)
    return top, (value - top.astype(F32)).astype(BF16)


def iota(shape, dim):
    return lax.broadcasted_iota(I32, shape, dim)


def ones_where(mask):
    return jnp.where(mask, 1.0, 0.0).astype(BF16)


def dot(a, b, ca=1, cb=0):
    return lax.dot_general(a, b, (((ca,), (cb,)), ((), ())), preferred_element_type=F32)


def widen(column, width):
    return jnp.concatenate([column] * (width // column.shape[1]), axis=1)


def as_column(row):
    parts = [
        jnp.broadcast_to(row[:, k : k + LANES], (LANES, LANES)).T
        for k in range(0, row.shape[1], LANES)
    ]
    return jnp.concatenate(parts, axis=0)


def whole():
    return pl.BlockSpec(memory_space=pltpu.VMEM)


def rows_of(tile, width):
    return pl.BlockSpec((tile, width), lambda i: (i, 0))


def fixed(shape):
    return pl.BlockSpec(shape, lambda i: (0, 0), pipeline_mode=pl.Buffered(1))


def lanes_of(height, tile):
    return pl.BlockSpec((height, tile), lambda i: (0, i))


def in_hbm(array):
    return pltpu.with_memory_space_constraint(array, pltpu.HBM)


def in_vmem(array):
    return pltpu.with_memory_space_constraint(array, pltpu.VMEM)


def sent_rows(cap):
    return cap * 3 // 4 if cap == GROUP else cap


def group_rows(t, sent):
    return pl.ds(0, sent) if sent < GROUP else pl.ds(pl.multiple_of(t * GROUP, GROUP), GROUP)


def put_parts(out, chunk, value):
    rows = value.shape[0]
    at = 0 if chunk is None else pl.multiple_of(chunk * 2 * rows, 2 * rows)
    out[pl.ds(at, rows), :], out[pl.ds(at + rows, rows), :] = two_parts(value)


def twice(mask, chunk):
    parts = []
    for k in range(0, mask.shape[1], chunk):
        parts += [mask[:, k : k + chunk]] * 2
    return jnp.concatenate(parts, axis=1)


def params(mib):
    return pltpu.CompilerParams(vmem_limit_bytes=mib * MIB)


def rank_entries(entry, rank_ref, note, cap):
    rows = entry.shape[1]
    high = rows // LANES
    place = entry + rows
    crosses = place < rows
    high_hit = ones_where((iota((high, rows), 0) == (place >> 7)) & crosses)
    low_hit = jnp.where((iota((LANES, rows), 0) == (place & (LANES - 1))) & crosses, 1.0, 0.0)
    present = ones_where(dot(high_hit, low_hit.astype(BF16), 1, 1) > 0.5)
    square = (LANES, LANES)
    within = dot(present, ones_where(iota(square, 0) < iota(square, 1)))
    small = (high, high)
    ahead = dot(ones_where(iota(small, 1) < iota(small, 0)), present)
    table = within + jnp.sum(ahead, axis=1, keepdims=True)
    table_high = jnp.floor(table * (1.0 / 256.0))
    table_low = table - 256.0 * table_high
    found = 256.0 * dot(table_high.astype(BF16), high_hit, 0, 0)
    found = found + dot(table_low.astype(BF16), high_hit, 0, 0)
    rank = jnp.sum(found * low_hit, axis=0, keepdims=True)
    rank_ref[...] = jnp.where(crosses, rank.astype(I32), -1)
    count = jnp.sum(present.astype(F32))
    note[...] = jnp.where(iota(note.shape, 0) == 1, jnp.where(count > sent_rows(cap), 1.0, 0.0), 0.0)


def trunk_kernel(
    cap, block_start, entry_ref, x_ref, events_ref, byte_ref, shift_ref, w_in, w_mid, w_out,
    first_hidden, hidden, slope_in, slope_mid, indicator_out, weight, send, note,
    rank_ref,
):
    step = pl.program_id(0)
    tile = x_ref.shape[0]

    @pl.when(step == 0)
    def _():
        rank_entries(entry_ref[...] - block_start[0], rank_ref, note, cap)
        send[...] = jnp.zeros_like(send)

    events = events_ref[...]
    split = jnp.concatenate([events & 255, events >> 8], axis=0).astype(F32).astype(BF16)
    spread = dot(split, byte_ref[...], 0, 0)
    bits = jnp.bitwise_and(jnp.right_shift(spread.astype(I32), shift_ref[...]), 1)
    indicator = bits.astype(F32)
    indicator_out[...] = indicator.astype(BF16)

    preact = dot(x_ref[...], w_in[...])
    sigma = jax.nn.sigmoid(preact)
    first = (preact * sigma).astype(BF16)
    first_hidden[...] = first
    slope_in[...] = sigma * (1.0 + preact * (1.0 - sigma))
    mid_pre = dot(first, w_mid[...])
    sigma = jax.nn.sigmoid(mid_pre)
    second = (mid_pre * sigma).astype(BF16)
    hidden[...] = second
    slope_mid[...] = sigma * (1.0 + mid_pre * (1.0 - sigma))
    log_hazard = dot(second, w_out[...])
    put_parts(weight, None, jnp.exp(log_hazard))
    note[0:1, :] -= jnp.sum(indicator * log_hazard, axis=0, keepdims=True)

    sent = sent_rows(cap)
    own = pl.ds(pl.multiple_of(step * tile, tile), tile)
    rank = rank_ref[:, own]
    entry = (entry_ref[:, own] - block_start[0] + rank_ref.shape[1]).astype(F32)

    def total(t, _):
        hit = iota((GROUP, tile), 0) + t * GROUP == rank
        place = jnp.max(jnp.where(hit, entry, 0.0), axis=1, keepdims=True)
        place = jnp.broadcast_to(place, (GROUP, LANES))
        parts = [place[k : k + LANES, :].T[0:1] for k in range(0, GROUP, LANES)]
        spot = (send.shape[0] - sent, GROUP)
        place = jnp.broadcast_to(jnp.concatenate(parts, axis=1), spot)
        place = jnp.where(iota(spot, 0) == t, place, 0.0)
        send[sent:, 0:GROUP] = jnp.maximum(send[sent:, 0:GROUP], place)
        at = group_rows(t, sent)
        hit = ones_where(hit)[: min(GROUP, sent)]
        send[at, :] += dot(twice(hit, tile), weight[...])
        return 0

    lax.fori_loop(0, cap // GROUP, total, 0)


def trunk(cap, block_start, entry, features, events, w_in, w_mid, w_out):
    rows, width = features.shape
    mid = w_in.shape[1]
    wide = w_mid.shape[1]
    out_width = w_out.shape[1]
    words = events.shape[1]
    column = np.arange(out_width)
    owner = (np.arange(words)[:, None] == column // BITS).astype(np.float32)
    bit = column % BITS
    byte = jnp.asarray(np.concatenate([owner * (bit < 8), owner * (bit >= 8)]), BF16)
    shift = jnp.asarray((bit % 8)[None, :], I32)
    sent = sent_rows(cap) + -(-(cap // GROUP) // 8) * 8
    constant = (byte, shift, w_in, w_mid, w_out)
    like = jax.ShapeDtypeStruct
    return pl.pallas_call(
        partial(trunk_kernel, cap),
        grid=(rows // TILE,),
        in_specs=[
            pl.BlockSpec(memory_space=pltpu.SMEM), fixed((1, rows)), rows_of(TILE, width),
            lanes_of(words, TILE),
        ]
        + [fixed(a.shape) for a in constant],
        out_specs=[
            rows_of(TILE, mid), rows_of(TILE, wide), rows_of(TILE, mid), rows_of(TILE, wide),
            rows_of(TILE, out_width), rows_of(2 * TILE, out_width),
        ]
        + [whole()] * 3,
        out_shape=[
            pltpu.HBM((rows, mid), BF16), pltpu.HBM((rows, wide), BF16),
            pltpu.HBM((rows, mid), F32), pltpu.HBM((rows, wide), F32),
            pltpu.HBM((rows, out_width), BF16), pltpu.HBM((2 * rows, out_width), BF16),
            like((sent, out_width), F32),
            like((8, out_width), F32), like((1, rows), I32),
        ],
        compiler_params=params(28),
        name="trunk",
    )(block_start, *map(in_hbm, (entry, features, events.T, *constant)))


def parts_at(array, row, count):
    if count == DEPTH:
        return array[pl.ds(pl.multiple_of(row * 2, 2 * DEPTH), 2 * DEPTH), :]
    at = row + row // DEPTH * DEPTH
    top = array[pl.ds(pl.multiple_of(at, count), count), :]
    rest = array[pl.ds(pl.multiple_of(at + DEPTH, count), count), :]
    return jnp.concatenate([top, rest], axis=0)


def own_risk_kernel(starts, entry_ref, first_ref, weight, out):
    step = pl.program_id(0)
    tile = first_ref.shape[1]
    rows = weight.shape[0] // 2
    first = as_column(first_ref[...])
    own = pl.ds(pl.multiple_of(step * tile, tile), tile)

    def part(at, count):
        at = pl.multiple_of(at, count)
        row = iota((tile, count), 1) + at
        wide = widen(first, count)
        mask = ones_where((row >= wide) & (entry_ref[:, pl.ds(at, count)] <= wide))
        return dot(twice(mask, count), parts_at(weight, at, count))

    def ahead(k, _):
        out[own, :] += part(k * LANES, LANES)
        return 0

    def behind(k, _):
        out[own, :] += part(k * DEPTH, DEPTH)
        return 0

    out[own, :] = part(step * tile, tile)
    lax.fori_loop(starts[step * (tile // LANES)] // LANES, step * (tile // LANES), ahead, 0)
    lax.fori_loop(step + 1, rows // DEPTH, behind, 0)


def block_sum(flops):
    return pl.CostEstimate(flops=flops, bytes_accessed=flops // 256, transcendentals=0)


def own_risk(starts, entry, first, weight):
    rows, width = weight.shape[0] // 2, weight.shape[1]
    return pl.pallas_call(
        own_risk_kernel,
        grid=(rows // TILE,),
        in_specs=[
            pl.BlockSpec(memory_space=pltpu.SMEM), whole(), lanes_of(1, TILE),
            fixed(weight.shape),
        ],
        out_specs=whole(),
        out_shape=pltpu.VMEM((rows, width), F32),
        compiler_params=params(16),
        cost_estimate=block_sum(rows * rows * width * 4),
        name="own_risk",
    )(starts, entry, first, in_hbm(weight))


def own_exposure_kernel(starts, first_ref, entry_ref, hazard, out, note):
    step = pl.program_id(0)
    tile = entry_ref.shape[1]

    @pl.when(step == 0)
    def _():
        note[...] = jnp.zeros_like(note)

    entry = as_column(entry_ref[...])
    own = pl.ds(pl.multiple_of(step * tile, tile), tile)
    end = (step + 1) * tile
    reach = jnp.int32(0)
    for k in range(first_ref.shape[1] // LANES):
        inside = (k * LANES >= end) & (starts[k] < end)
        reach += jnp.where(inside, 1, 0).astype(I32)

    def part(at, count):
        at = pl.multiple_of(at, count)
        first = first_ref[:, pl.ds(at, count)]
        row = iota((tile, count), 0) + step * tile
        mask = ones_where((first >= widen(entry, count)) & (first <= row))
        return dot(twice(mask, count), parts_at(hazard, at, count))

    def before(k, _):
        out[own, :] += part(k * DEPTH, DEPTH)
        return 0

    def after(k, _):
        out[own, :] += part(end + k * LANES, LANES)
        return 0

    out[own, :] = part(step * tile, tile)
    top = hazard[pl.ds(pl.multiple_of(step * 2 * tile, tile), tile), :].astype(F32)
    rest = hazard[pl.ds(pl.multiple_of(step * 2 * tile + tile, tile), tile), :].astype(F32)
    logs = jnp.where(top > 0.0, jnp.log(top + rest), 0.0)
    note[0:1, :] -= jnp.sum(logs, axis=0, keepdims=True)
    lax.fori_loop(0, step, before, 0)
    lax.fori_loop(0, reach, after, 0)


def own_exposure(starts, first, entry, hazard):
    rows, width = hazard.shape[0] // 2, hazard.shape[1]
    like = jax.ShapeDtypeStruct
    return pl.pallas_call(
        own_exposure_kernel,
        grid=(rows // TILE,),
        in_specs=[
            pl.BlockSpec(memory_space=pltpu.SMEM), whole(), lanes_of(1, TILE), whole()
        ],
        out_specs=[whole(), whole()],
        out_shape=[pltpu.VMEM((rows, width), F32), like((8, width), F32)],
        compiler_params=params(12),
        cost_estimate=block_sum(rows * rows * width * 4),
        name="own_exposure",
    )(starts, first, entry, in_vmem(hazard))


def split_sum(source, parts, cap):
    sent = sent_rows(cap)
    for t in range(cap // GROUP):
        rows = min(GROUP, sent - t * GROUP)
        value = source[t * GROUP : t * GROUP + rows, :]
        if rows < GROUP:
            value = jnp.concatenate([value, jnp.zeros((GROUP - rows, value.shape[1]), F32)], axis=0)
        put_parts(parts, t, value)


def group_sum(mask, parts, t):
    at = pl.ds(pl.multiple_of(t * 2 * GROUP, 2 * GROUP), 2 * GROUP)
    return dot(twice(mask, GROUP), parts[at, :])


def hazard_kernel(
    cap, first_all, first_ref, risk, indicator_ref, got, hazard, sums, parts
):
    step = pl.program_id(0)
    tile = first_ref.shape[1]
    rows = hazard.shape[0] // 2
    own = pl.ds(pl.multiple_of(step * tile, tile), tile)

    @pl.when(step == 0)
    def _():
        split_sum(got, parts, cap)

    first = widen(as_column(first_ref[...]).astype(F32), GROUP)
    divisor = risk[own, :]
    sent = sent_rows(cap)

    def beyond(t, total):
        entry = got[pl.ds(sent + t, 1), 0:GROUP]
        return total + group_sum(ones_where(entry <= first), parts, t)

    divisor = lax.fori_loop(0, cap // GROUP, beyond, divisor)
    put_parts(hazard, step, indicator_ref[...].astype(F32) / divisor)

    @pl.when(step == pl.num_programs(0) - 1)
    def _():
        def total(t, _):
            entry = as_column(got[pl.ds(sent + t, 1), 0:GROUP])[: min(GROUP, sent)]
            entry = widen(entry, rows)
            mask = ones_where(first_all[...].astype(F32) >= entry)
            sums[group_rows(t, sent), :] = dot(twice(mask, DEPTH), hazard[...])
            return 0

        lax.fori_loop(0, cap // GROUP, total, 0)


def hazards(cap, first, risk, indicator, got):
    rows, width = risk.shape
    like = jax.ShapeDtypeStruct
    return pl.pallas_call(
        partial(hazard_kernel, cap),
        grid=(rows // TILE,),
        in_specs=[
            whole(), lanes_of(1, TILE), whole(), rows_of(TILE, width), whole()
        ],
        out_specs=[whole(), whole()],
        out_shape=[pltpu.VMEM((2 * rows, width), BF16), like((sent_rows(cap), width), F32)],
        scratch_shapes=[pltpu.VMEM((2 * cap, width), BF16)],
        compiler_params=params(20),
        name="hazards",
    )(first, first, in_vmem(risk), in_hbm(indicator), got)


def backward_kernel(
    cap, factor, half, rank_ref, exposure_ref, got, note, log_part, weight, indicator, hidden,
    slope_mid, first_hidden, slope_in, x_ref, w_in, w_mid, w_out, grad_x, keep, send,
    parts, grad_in, grad_mid, grad_out,
):
    step = pl.program_id(0)
    tile = rank_ref.shape[1]
    own = pl.ds(pl.multiple_of(step * tile, tile), tile)

    @pl.when(step == 0)
    def _():
        split_sum(got, parts, cap)
        grad_in[...] = jnp.zeros_like(grad_in)
        grad_mid[...] = jnp.zeros_like(grad_mid)
        grad_out[...] = jnp.zeros_like(grad_out)

    rank = widen(as_column(rank_ref[...]), GROUP)

    def behind(t, total):
        return total + group_sum(ones_where(rank == iota((tile, GROUP), 1) + t * GROUP), parts, t)

    exposure = lax.fori_loop(0, cap // GROUP, behind, exposure_ref[own, :])
    part = tile // 2
    cuts = [slice(0, part), slice(part, tile)]
    at = [pl.ds(pl.multiple_of(step * tile + k * part, part), part) for k in range(2)]
    etas = []
    for k in range(2):
        start = step * 2 * tile + k * part
        top = weight[pl.ds(pl.multiple_of(start, part), part), :].astype(F32)
        rest = weight[pl.ds(pl.multiple_of(start + tile, part), part), :].astype(F32)
        value = (top + rest) * exposure[cuts[k]] - indicator[at[k], :].astype(F32)
        etas.append(value.astype(BF16))
    mids = [dot(eta, w_out[...], 1, 1) for eta in etas]
    grad_out[...] += dot(hidden[own, :], jnp.concatenate(etas, axis=0), 0, 0)
    mids = [(mids[k] * slope_mid[at[k], :]).astype(BF16) for k in range(2)]
    pres = [dot(mid, w_mid[...], 1, 1) for mid in mids]
    grad_mid[...] += dot(first_hidden[own, :], jnp.concatenate(mids, axis=0), 0, 0)
    pres = [(pres[k] * slope_in[at[k], :]).astype(BF16) for k in range(2)]
    grad_in[...] += dot(x_ref[own, :], jnp.concatenate(pres, axis=0), 0, 0)
    for k in range(2):
        grad_x[cuts[k], :] = dot(pres[k], w_in[...], 1, 1).astype(BF16)

    @pl.when(step == pl.num_programs(0) - 1)
    def _():
        body, rest = grad_mid.shape[0], grad_out.shape[0] // 2
        end = body + rest

        def write(out, block, at):
            out[0:body, :] = block[...] * factor
            out[body:end, :] = grad_out[at : at + rest, :] * factor
            out[end:, :] = note[...] + log_part[...]

        @pl.when(half[0] == 0)
        def _():
            write(keep, grad_mid, 0)
            write(send, grad_in, rest)

        @pl.when(half[0] != 0)
        def _():
            write(keep, grad_in, rest)
            write(send, grad_mid, 0)


def backward(cap, factor, half, rank, exposure, got, notes, kept, features, w_in, w_mid, w_out):
    rows, width = features.shape
    out_width = exposure.shape[1]
    halves = (w_mid.shape[0] + w_out.shape[0] // 2 + 8, out_width)
    tiles = [in_vmem(a) for a in (*kept, features)]
    weights = (w_in, w_mid, w_out)
    return pl.pallas_call(
        partial(backward_kernel, cap, factor),
        grid=(rows // TILE,),
        in_specs=[pl.BlockSpec(memory_space=pltpu.SMEM), lanes_of(1, TILE)]
        + [whole()] * (2 + len(notes))
        + [whole()] * (len(tiles) + 3),
        out_specs=[rows_of(TILE, width), whole(), whole()],
        out_shape=[
            pltpu.HBM((rows, width), BF16), pltpu.HBM(halves, F32),
            jax.ShapeDtypeStruct(halves, F32),
        ],
        scratch_shapes=[pltpu.VMEM((2 * cap, out_width), BF16)]
        + [pltpu.VMEM(w.shape, F32) for w in weights],
        compiler_params=params(20),
        name="backward",
    )(half, rank, in_vmem(exposure), got, *notes, *tiles, *weights)


def in_steps(rows, work):
    step = 16 if rows % 16 == 0 else 8
    if rows <= step:
        work(0, rows)
        return

    def body(k, _):
        work(pl.multiple_of(k * step, 8), step)
        return 0

    lax.fori_loop(0, rows // step, body, 0, unroll=2)


def spread_kernel(sizes, streams, fetch, me, *refs):
    count = sum(sizes)
    outs = iter(refs[count:])
    if fetch:
        held, sems = refs[-1 - count : -1], refs[-1]
        copies = [
            pltpu.make_async_copy(refs[i], held[i], sems.at[i]) for i in range(count)
        ]
        for copy in copies:
            copy.start()
        for copy in copies:
            copy.wait()
        refs = held
    groups_of = []
    for size in sizes:
        groups_of.append(refs[:size])
        refs = refs[size:]

    def total(which, rows):
        value = groups_of[which][0][rows, :]
        for ref in groups_of[which][1:]:
            value = value + ref[rows, :]
        return value

    for i, (which, at, rows, tail_at, tail, groups) in enumerate(streams):
        if not groups:
            flag = jnp.max(total(which, pl.ds(at, rows)))
            next(outs)[0] = jnp.where(flag > 0.0, 1, 0).astype(I32)
            continue
        piece = rows // groups
        for m in range(groups):
            out = next(outs)
            begin = at
            if groups > 1:
                begin = pl.multiple_of(at + jnp.bitwise_xor(me[i], m) * piece, 8)

            def work(row, step, out=out, begin=begin):
                source = pl.ds(pl.multiple_of(begin + row, 8), step)
                out[pl.ds(row, step), :] = total(which, source)

            in_steps(piece, work)
            if tail:
                out[piece : piece + tail, :] = total(which, pl.ds(tail_at, tail))


def spread(terms, streams, me, name, fetch=False):
    width = terms[0][0].shape[1]
    shapes, places = [], []
    for _, _, rows, _, tail, groups in streams:
        if groups:
            shapes += [pltpu.VMEM((rows // groups + tail, width), F32)] * groups
            places += [pl.BlockSpec(memory_space=pltpu.VMEM)] * groups
        else:
            shapes.append(jax.ShapeDtypeStruct((1,), I32))
            places.append(pl.BlockSpec(memory_space=pltpu.SMEM))
    flat = [a for term in terms for a in term]
    scratch = [pltpu.VMEM(a.shape, F32) for a in flat] + [pltpu.SemaphoreType.DMA((len(flat),))]
    out = pl.pallas_call(
        partial(spread_kernel, [len(term) for term in terms], streams, fetch),
        in_specs=[pl.BlockSpec(memory_space=pltpu.SMEM)]
        + [pl.BlockSpec(memory_space=pl.ANY if fetch else pltpu.VMEM)] * len(flat),
        out_specs=places,
        out_shape=shapes,
        scratch_shapes=scratch if fetch else [],
        compiler_params=params(16),
        name=name,
    )(me, *flat)
    parts = []
    for stream in streams:
        parts.append(out[: max(stream[-1], 1)])
        out = out[max(stream[-1], 1) :]
    return parts


def collect_kernel(places, me, *refs):
    count = sum(groups for groups, _, _ in places)
    outs = refs[count:]
    start = 0
    for i, (groups, which, at) in enumerate(places):
        piece = refs[start].shape[0]
        for m in range(groups):
            begin = pl.multiple_of(at + jnp.bitwise_xor(me[i], m) * piece, 8)

            def work(row, step, out=outs[which], ref=refs[start + m], begin=begin):
                target = pl.ds(pl.multiple_of(begin + row, 8), step)
                out[target, :] = ref[pl.ds(row, step), :]

            in_steps(piece, work)
        start += groups


def collect(streams, out_rows, me, name):
    flat = [a for pieces, _, _ in streams for a in pieces]
    width = flat[0].shape[1]
    return pl.pallas_call(
        partial(collect_kernel, [(len(pieces), which, at) for pieces, which, at in streams]),
        in_specs=[pl.BlockSpec(memory_space=pltpu.SMEM)]
        + [pl.BlockSpec(memory_space=pltpu.VMEM)] * len(flat),
        out_specs=[pl.BlockSpec(memory_space=pltpu.VMEM)] * len(out_rows),
        out_shape=[pltpu.VMEM((rows, width), F32) for rows in out_rows],
        compiler_params=params(16),
        name=name,
    )(me, *flat)


def plan(body, rest):
    strata, chain = lax.axis_size("strata"), lax.axis_size("chain")
    if strata % 2 or chain % 4 or strata & (strata - 1) or chain & (chain - 1):
        return None
    across = chain // 4
    plane, line = strata // 2 * across, 4
    if body % (8 * plane * line) or rest % (8 * line):
        return None
    return across, plane, line


def hop(block, strata_flip, chain_flip):
    strata, chain = lax.axis_size("strata"), lax.axis_size("chain")
    route = [
        (s * chain + c, (s ^ strata_flip) * chain + (c ^ chain_flip))
        for s in range(strata)
        for c in range(chain)
    ]
    return lax.ppermute(block, ("strata", "chain"), route)


def hops(groups):
    across, plane, line = groups
    strata, chain = lax.axis_index("strata"), lax.axis_index("chain")

    def plane_hops(pieces):
        return [pieces[0]] + [
            hop(pieces[m], m // across * 2, m % across) for m in range(1, plane)
        ]

    def line_hops(pieces):
        return [pieces[0]] + [hop(pieces[m], 0, m * across) for m in range(1, line)]

    return plane_hops, line_hops, strata // 2 * across + chain % across, chain // across


def reduced(keep, send, body, rest, groups):
    plane_hops, line_hops, in_plane, in_line = hops(groups)
    _, plane, line = groups
    end = body + rest
    tail = keep.shape[0] - end
    a, b = spread(
        [[in_hbm(keep), hop(send, 1, 0)]],
        [(0, 0, body, end, tail, plane), (0, body, rest, 0, 0, line)],
        jnp.stack([in_plane, in_line]), "spread_first", fetch=True,
    )
    a, b = plane_hops(a), line_hops(b)
    size_a, size_b = body // plane, rest // line
    none = jnp.zeros((3,), I32)
    ((b,),) = spread([b], [(0, 0, size_b, 0, 0, 1)], none, "lines_summed")
    (a,) = spread(
        [a], [(0, 0, size_a, size_a, tail, line)], in_line.reshape(1), "spread_second"
    )
    a, b = line_hops(a), plane_hops([b] * plane)
    ((b,),) = spread([b], [(0, 0, size_b, 0, 0, 1)], none, "rest_summed")
    size_a = size_a // line
    (a,), (note,), (flag,) = spread(
        [a],
        [(0, 0, size_a, 0, 0, 1), (0, size_a, tail, 0, 0, 1), (0, size_a + 1, 1, 0, 0, 0)],
        none, "body_summed",
    )
    (a,) = collect(
        [(line_hops([a] * line), 0, 0)], [body // plane], in_line.reshape(1), "collect_first"
    )
    return flag, note, a, b


def gathered(a, b, body, rest, groups):
    plane_hops, line_hops, in_plane, in_line = hops(groups)
    _, plane, line = groups
    a, b = plane_hops([a] * plane), line_hops([b] * line)
    (own,) = collect(
        [(a, 0, 0), (b, 0, body)], [body + rest], jnp.stack([in_plane, in_line]), "collect_second"
    )
    return own, hop(own, 1, 0)


def place_kernel(of_core, half, block, *refs):
    grad_in, grad_mid, grad_out, sems = refs[-4:]
    body, rest = grad_mid.shape[0], grad_out.shape[0] // 2

    def write(target, at):
        copies = [
            pltpu.make_async_copy(block.at[pl.ds(0, body)], target, sems.at[0]),
            pltpu.make_async_copy(
                block.at[pl.ds(body, rest)], grad_out.at[pl.ds(at, rest)], sems.at[1]
            ),
        ]
        for copy in copies:
            copy.start()
        for copy in copies:
            copy.wait()

    @pl.when(half[0] == of_core)
    def _():
        write(grad_mid, 0)

    @pl.when(half[0] != of_core)
    def _():
        write(grad_in, rest)


def place(of_core, half, block, shapes, results):
    somewhere = pl.BlockSpec(memory_space=pl.ANY)
    return pl.pallas_call(
        partial(place_kernel, of_core),
        in_specs=[
            pl.BlockSpec(memory_space=pltpu.SMEM), pl.BlockSpec(memory_space=pltpu.VMEM)
        ]
        + [somewhere] * len(results),
        out_specs=[somewhere] * 3,
        out_shape=[pltpu.HBM(shape, F32) for shape in shapes],
        scratch_shapes=[pltpu.SemaphoreType.DMA((2,))],
        input_output_aliases={2 + i: i for i in range(len(results))},
        compiler_params=params(16),
        name="place",
    )(half, block, *results)


def finish(half, own, got, shapes):
    results = place(0, half, own, shapes, ())
    return place(1, half, got, shapes, results)


def from_behind(block, axis, distance):
    devices = range(lax.axis_size(axis))
    route = [(i - distance, i) for i in devices if i - distance in devices]
    return lax.ppermute(block, axis, route)


def pipeline(cap, total_rows, half, features, events, tie_first, entry_row, w_in, w_mid, w_out):
    rows = features.shape[0]
    block_start = (lax.axis_index("chain") * rows).reshape(1)
    first = tie_first - block_start
    entry = entry_row - block_start
    first_line = first.reshape(1, rows)
    entry_line = entry.reshape(1, rows)
    starts = first[::LANES]
    (
        first_hidden, hidden, slope_in, slope_mid, indicator, weight, send, note, rank,
    ) = trunk(
        cap, block_start, entry_row.reshape(1, rows), features, events, w_in, w_mid, w_out
    )
    got = from_behind(send, "chain", -1)
    risk = own_risk(starts, entry_line, first_line, weight)
    hazard, sums = hazards(cap, first_line, risk, indicator, got)
    got_sums = from_behind(sums, "chain", 1)
    exposure, log_part = own_exposure(starts, first_line, entry_line, hazard)
    kept = (weight, indicator, hidden, slope_mid, first_hidden, slope_in)
    return backward(
        cap, total_rows ** (-0.5), half, rank, exposure, got_sums, (note, log_part), kept,
        features, w_in, w_mid, w_out,
    )


def on_device(features, events, tie_first, entry_row, w_in, w_mid, w_out):
    rows = features.shape[0]
    total_rows = rows * lax.axis_size("chain") * lax.axis_size("strata")
    args = (features, events, tie_first, entry_row, w_in, w_mid, w_out)
    shapes = (w_in.shape, w_mid.shape, w_out.shape)
    body, rest = w_mid.shape[0], w_out.shape[0] // 2
    end = body + rest
    groups = plan(body, rest)
    half = jnp.zeros((1,), I32)
    if groups:
        half = half + lax.axis_index("strata") % 2

    def run(cap):
        grad_x, keep, send = pipeline(cap, total_rows, half, *args)
        if groups:
            flag, note, a, b = reduced(keep, send, body, rest, groups)
        else:
            a, b = lax.psum((keep, send[:end]), ("strata", "chain"))
            a, note = a[:end], a[end:]
            flag = (note[1, 0:1] > 0).astype(I32)
        return flag, note, grad_x, a, b

    _, note, grad_x, a, b = lax.while_loop(
        lambda state: state[0][0] > 0, lambda _: run(rows), run(min(GROUP, rows))
    )
    own, other = gathered(a, b, body, rest, groups) if groups else (a, b)
    return (note[0] / total_rows, grad_x, *finish(half, own, other, shapes))


def solution(mesh):
    placed = (
        P(("strata", "chain"), None),
        P(("strata", "chain"), None),
        P(("strata", "chain")),
        P(("strata", "chain")),
        P(),
        P(),
        P(),
    )
    return jax.shard_map(
        on_device,
        mesh=mesh,
        in_specs=placed,
        out_specs=(P(), P(("strata", "chain"), None), P(), P(), P()),
        check_vma=False,
    )
```

```python
from functools import partial

import jax
import jax.numpy as jnp
import numpy as np
from jax import lax
from jax.experimental import pallas as pl
from jax.experimental.pallas import tpu as pltpu
from jax.sharding import PartitionSpec as P

BITS = 15
LANES = 128
TILE = 512
DEPTH = 512
GROUP = 256
MIB = 1024 * 1024
F32 = jnp.float32
BF16 = jnp.bfloat16
I32 = jnp.int32


def two_parts(value):
    top = value.astype(BF16)
    return top, (value - top.astype(F32)).astype(BF16)


def iota(shape, dim):
    return lax.broadcasted_iota(I32, shape, dim)


def ones_where(mask):
    return jnp.where(mask, 1.0, 0.0).astype(BF16)


def dot(a, b, ca=1, cb=0):
    return lax.dot_general(a, b, (((ca,), (cb,)), ((), ())), preferred_element_type=F32)


def widen(column, width):
    return jnp.concatenate([column] * (width // column.shape[1]), axis=1)


def as_column(row):
    parts = [
        jnp.broadcast_to(row[:, k : k + LANES], (LANES, LANES)).T
        for k in range(0, row.shape[1], LANES)
    ]
    return jnp.concatenate(parts, axis=0)


def whole():
    return pl.BlockSpec(memory_space=pltpu.VMEM)


def rows_of(tile, width):
    return pl.BlockSpec((tile, width), lambda i: (i, 0))


def fixed(shape):
    return pl.BlockSpec(shape, lambda i: (0, 0), pipeline_mode=pl.Buffered(1))


def lanes_of(height, tile):
    return pl.BlockSpec((height, tile), lambda i: (0, i))


def in_hbm(array):
    return pltpu.with_memory_space_constraint(array, pltpu.HBM)


def in_vmem(array):
    return pltpu.with_memory_space_constraint(array, pltpu.VMEM)


def sent_rows(cap):
    return cap * 3 // 4 if cap == GROUP else cap


def group_rows(t, sent):
    return pl.ds(0, sent) if sent < GROUP else pl.ds(pl.multiple_of(t * GROUP, GROUP), GROUP)


def put_parts(out, chunk, value):
    rows = value.shape[0]
    at = 0 if chunk is None else pl.multiple_of(chunk * 2 * rows, 2 * rows)
    out[pl.ds(at, rows), :], out[pl.ds(at + rows, rows), :] = two_parts(value)


def twice(mask, chunk):
    parts = []
    for k in range(0, mask.shape[1], chunk):
        parts += [mask[:, k : k + chunk]] * 2
    return jnp.concatenate(parts, axis=1)


def params(mib):
    return pltpu.CompilerParams(vmem_limit_bytes=mib * MIB)


def rank_entries(entry, rank_ref, note, cap):
    rows = entry.shape[1]
    high = rows // LANES
    place = entry + rows
    crosses = place < rows
    high_hit = ones_where((iota((high, rows), 0) == (place >> 7)) & crosses)
    low_hit = jnp.where((iota((LANES, rows), 0) == (place & (LANES - 1))) & crosses, 1.0, 0.0)
    present = ones_where(dot(high_hit, low_hit.astype(BF16), 1, 1) > 0.5)
    square = (LANES, LANES)
    within = dot(present, ones_where(iota(square, 0) < iota(square, 1)))
    small = (high, high)
    ahead = dot(ones_where(iota(small, 1) < iota(small, 0)), present)
    table = within + jnp.sum(ahead, axis=1, keepdims=True)
    table_high = jnp.floor(table * (1.0 / 256.0))
    table_low = table - 256.0 * table_high
    found = 256.0 * dot(table_high.astype(BF16), high_hit, 0, 0)
    found = found + dot(table_low.astype(BF16), high_hit, 0, 0)
    rank = jnp.sum(found * low_hit, axis=0, keepdims=True)
    rank_ref[...] = jnp.where(crosses, rank.astype(I32), -1)
    count = jnp.sum(present.astype(F32))
    note[...] = jnp.where(iota(note.shape, 0) == 1, jnp.where(count > sent_rows(cap), 1.0, 0.0), 0.0)


def trunk_kernel(
    cap, block_start, entry_ref, x_ref, events_ref, byte_ref, shift_ref, w_in, w_mid, w_out,
    first_hidden, hidden, slope_in, slope_mid, indicator_out, weight, send, note,
    rank_ref,
):
    step = pl.program_id(0)
    tile = x_ref.shape[0]

    @pl.when(step == 0)
    def _():
        rank_entries(entry_ref[...] - block_start[0], rank_ref, note, cap)
        send[...] = jnp.zeros_like(send)

    events = events_ref[...]
    split = jnp.concatenate([events & 255, events >> 8], axis=0).astype(F32).astype(BF16)
    spread = dot(split, byte_ref[...], 0, 0)
    bits = jnp.bitwise_and(jnp.right_shift(spread.astype(I32), shift_ref[...]), 1)
    indicator = bits.astype(F32)
    indicator_out[...] = indicator.astype(BF16)

    preact = dot(x_ref[...], w_in[...])
    sigma = jax.nn.sigmoid(preact)
    first = (preact * sigma).astype(BF16)
    first_hidden[...] = first
    slope_in[...] = sigma * (1.0 + preact * (1.0 - sigma))
    mid_pre = dot(first, w_mid[...])
    sigma = jax.nn.sigmoid(mid_pre)
    second = (mid_pre * sigma).astype(BF16)
    hidden[...] = second
    slope_mid[...] = sigma * (1.0 + mid_pre * (1.0 - sigma))
    log_hazard = dot(second, w_out[...])
    put_parts(weight, None, jnp.exp(log_hazard))
    note[0:1, :] -= jnp.sum(indicator * log_hazard, axis=0, keepdims=True)

    sent = sent_rows(cap)
    own = pl.ds(pl.multiple_of(step * tile, tile), tile)
    rank = rank_ref[:, own]
    entry = (entry_ref[:, own] - block_start[0] + rank_ref.shape[1]).astype(F32)

    def total(t, _):
        hit = iota((GROUP, tile), 0) + t * GROUP == rank
        place = jnp.max(jnp.where(hit, entry, 0.0), axis=1, keepdims=True)
        place = jnp.broadcast_to(place, (GROUP, LANES))
        if sent < GROUP:
            place = jnp.concatenate([place[:sent]] * 2, axis=0)
        width = place.shape[0]
        parts = [place[k : k + LANES, :].T[0:1] for k in range(0, width, LANES)]
        spot = (send.shape[0] - sent, width)
        place = jnp.broadcast_to(jnp.concatenate(parts, axis=1), spot)
        place = jnp.where(iota(spot, 0) == t, place, 0.0)
        send[sent:, 0:width] = jnp.maximum(send[sent:, 0:width], place)
        at = group_rows(t, sent)
        hit = ones_where(hit)[: min(GROUP, sent)]
        send[at, :] += dot(twice(hit, tile), weight[...])
        return 0

    lax.fori_loop(0, cap // GROUP, total, 0)


def trunk(cap, block_start, entry, features, events, w_in, w_mid, w_out):
    rows, width = features.shape
    mid = w_in.shape[1]
    wide = w_mid.shape[1]
    out_width = w_out.shape[1]
    words = events.shape[1]
    column = np.arange(out_width)
    owner = (np.arange(words)[:, None] == column // BITS).astype(np.float32)
    bit = column % BITS
    byte = jnp.asarray(np.concatenate([owner * (bit < 8), owner * (bit >= 8)]), BF16)
    shift = jnp.asarray((bit % 8)[None, :], I32)
    sent = sent_rows(cap) + -(-(cap // GROUP) // 8) * 8
    constant = (byte, shift, w_in, w_mid, w_out)
    like = jax.ShapeDtypeStruct
    return pl.pallas_call(
        partial(trunk_kernel, cap),
        grid=(rows // TILE,),
        in_specs=[
            pl.BlockSpec(memory_space=pltpu.SMEM), fixed((1, rows)), rows_of(TILE, width),
            lanes_of(words, TILE),
        ]
        + [fixed(a.shape) for a in constant],
        out_specs=[
            rows_of(TILE, mid), rows_of(TILE, wide), rows_of(TILE, mid), rows_of(TILE, wide),
            rows_of(TILE, out_width), rows_of(2 * TILE, out_width),
        ]
        + [whole()] * 3,
        out_shape=[
            pltpu.HBM((rows, mid), BF16), pltpu.HBM((rows, wide), BF16),
            pltpu.HBM((rows, mid), F32), pltpu.HBM((rows, wide), F32),
            pltpu.HBM((rows, out_width), BF16), pltpu.HBM((2 * rows, out_width), BF16),
            like((sent, out_width), F32),
            like((8, out_width), F32), like((1, rows), I32),
        ],
        compiler_params=params(28),
        name="trunk",
    )(block_start, *map(in_hbm, (entry, features, events.T, *constant)))


def parts_at(array, row, count):
    if count == DEPTH:
        return array[pl.ds(pl.multiple_of(row * 2, 2 * DEPTH), 2 * DEPTH), :]
    at = row + row // DEPTH * DEPTH
    top = array[pl.ds(pl.multiple_of(at, count), count), :]
    rest = array[pl.ds(pl.multiple_of(at + DEPTH, count), count), :]
    return jnp.concatenate([top, rest], axis=0)


def own_risk_kernel(starts, entry_ref, first_ref, weight, out):
    step = pl.program_id(0)
    tile = first_ref.shape[1]
    rows = weight.shape[0] // 2
    first = as_column(first_ref[...])
    own = pl.ds(pl.multiple_of(step * tile, tile), tile)

    def part(at, count):
        at = pl.multiple_of(at, count)
        row = iota((tile, count), 1) + at
        wide = widen(first, count)
        mask = ones_where((row >= wide) & (entry_ref[:, pl.ds(at, count)] <= wide))
        return dot(twice(mask, count), parts_at(weight, at, count))

    def ahead(k, _):
        out[own, :] += part(k * LANES, LANES)
        return 0

    def behind(k, _):
        out[own, :] += part(k * DEPTH, DEPTH)
        return 0

    out[own, :] = part(step * tile, tile)
    lax.fori_loop(starts[step * (tile // LANES)] // LANES, step * (tile // LANES), ahead, 0)
    lax.fori_loop(step + 1, rows // DEPTH, behind, 0)


def block_sum(flops):
    return pl.CostEstimate(flops=flops, bytes_accessed=flops // 256, transcendentals=0)


def own_risk(starts, entry, first, weight):
    rows, width = weight.shape[0] // 2, weight.shape[1]
    return pl.pallas_call(
        own_risk_kernel,
        grid=(rows // TILE,),
        in_specs=[
            pl.BlockSpec(memory_space=pltpu.SMEM), whole(), lanes_of(1, TILE),
            fixed(weight.shape),
        ],
        out_specs=whole(),
        out_shape=pltpu.VMEM((rows, width), F32),
        compiler_params=params(16),
        cost_estimate=block_sum(rows * rows * width * 4),
        name="own_risk",
    )(starts, entry, first, in_hbm(weight))


def own_exposure_kernel(starts, first_ref, entry_ref, hazard, out, note):
    step = pl.program_id(0)
    tile = entry_ref.shape[1]

    @pl.when(step == 0)
    def _():
        note[...] = jnp.zeros_like(note)

    entry = as_column(entry_ref[...])
    own = pl.ds(pl.multiple_of(step * tile, tile), tile)
    end = (step + 1) * tile
    reach = jnp.int32(0)
    for k in range(first_ref.shape[1] // LANES):
        inside = (k * LANES >= end) & (starts[k] < end)
        reach += jnp.where(inside, 1, 0).astype(I32)

    def part(at, count):
        at = pl.multiple_of(at, count)
        first = first_ref[:, pl.ds(at, count)]
        row = iota((tile, count), 0) + step * tile
        mask = ones_where((first >= widen(entry, count)) & (first <= row))
        return dot(twice(mask, count), parts_at(hazard, at, count))

    def before(k, _):
        out[own, :] += part(k * DEPTH, DEPTH)
        return 0

    def after(k, _):
        out[own, :] += part(end + k * LANES, LANES)
        return 0

    out[own, :] = part(step * tile, tile)
    top = hazard[pl.ds(pl.multiple_of(step * 2 * tile, tile), tile), :].astype(F32)
    rest = hazard[pl.ds(pl.multiple_of(step * 2 * tile + tile, tile), tile), :].astype(F32)
    logs = jnp.where(top > 0.0, jnp.log(top + rest), 0.0)
    note[0:1, :] -= jnp.sum(logs, axis=0, keepdims=True)
    lax.fori_loop(0, step, before, 0)
    lax.fori_loop(0, reach, after, 0)


def own_exposure(starts, first, entry, hazard):
    rows, width = hazard.shape[0] // 2, hazard.shape[1]
    like = jax.ShapeDtypeStruct
    return pl.pallas_call(
        own_exposure_kernel,
        grid=(rows // TILE,),
        in_specs=[
            pl.BlockSpec(memory_space=pltpu.SMEM), whole(), lanes_of(1, TILE), whole()
        ],
        out_specs=[whole(), whole()],
        out_shape=[pltpu.VMEM((rows, width), F32), like((8, width), F32)],
        compiler_params=params(12),
        cost_estimate=block_sum(rows * rows * width * 4),
        name="own_exposure",
    )(starts, first, entry, in_vmem(hazard))


def split_sum(source, parts, cap):
    sent = sent_rows(cap)
    group = min(GROUP, sent)
    for t in range(sent // group):
        put_parts(parts, t, source[t * group : (t + 1) * group, :])


def group_sum(column, test, parts, cap, t):
    sent = sent_rows(cap)
    if sent < GROUP:
        return dot(ones_where(test(widen(column, 2 * sent), 2 * sent)), parts[...])
    at = pl.ds(pl.multiple_of(t * 2 * GROUP, 2 * GROUP), 2 * GROUP)
    return dot(twice(ones_where(test(widen(column, GROUP), GROUP)), GROUP), parts[at, :])


def hazard_kernel(
    cap, first_all, first_ref, risk, indicator_ref, got, hazard, sums, parts
):
    step = pl.program_id(0)
    tile = first_ref.shape[1]
    rows = hazard.shape[0] // 2
    own = pl.ds(pl.multiple_of(step * tile, tile), tile)

    @pl.when(step == 0)
    def _():
        split_sum(got, parts, cap)

    first = as_column(first_ref[...]).astype(F32)
    divisor = risk[own, :]
    sent = sent_rows(cap)

    def beyond(t, total):
        def test(column, width):
            return got[pl.ds(sent + t, 1), 0:width] <= column

        return total + group_sum(first, test, parts, cap, t)

    divisor = lax.fori_loop(0, cap // GROUP, beyond, divisor)
    put_parts(hazard, step, indicator_ref[...].astype(F32) / divisor)

    @pl.when(step == pl.num_programs(0) - 1)
    def _():
        def total(t, _):
            entry = as_column(got[pl.ds(sent + t, 1), 0:GROUP])[: min(GROUP, sent)]
            entry = widen(entry, rows)
            mask = ones_where(first_all[...].astype(F32) >= entry)
            sums[group_rows(t, sent), :] = dot(twice(mask, DEPTH), hazard[...])
            return 0

        lax.fori_loop(0, cap // GROUP, total, 0)


def hazards(cap, first, risk, indicator, got):
    rows, width = risk.shape
    like = jax.ShapeDtypeStruct
    return pl.pallas_call(
        partial(hazard_kernel, cap),
        grid=(rows // TILE,),
        in_specs=[
            whole(), lanes_of(1, TILE), whole(), rows_of(TILE, width), whole()
        ],
        out_specs=[whole(), whole()],
        out_shape=[pltpu.VMEM((2 * rows, width), BF16), like((sent_rows(cap), width), F32)],
        scratch_shapes=[pltpu.VMEM((2 * sent_rows(cap), width), BF16)],
        compiler_params=params(20),
        name="hazards",
    )(first, first, in_vmem(risk), in_hbm(indicator), got)


def backward_kernel(
    cap, factor, half, rank_ref, exposure_ref, got, note, log_part, weight, indicator, hidden,
    slope_mid, first_hidden, slope_in, x_ref, w_in, w_mid, w_out, grad_x, keep, send,
    parts, grad_in, grad_mid, grad_out,
):
    step = pl.program_id(0)
    tile = rank_ref.shape[1]
    own = pl.ds(pl.multiple_of(step * tile, tile), tile)

    @pl.when(step == 0)
    def _():
        split_sum(got, parts, cap)
        grad_in[...] = jnp.zeros_like(grad_in)
        grad_mid[...] = jnp.zeros_like(grad_mid)
        grad_out[...] = jnp.zeros_like(grad_out)

    rank = as_column(rank_ref[...])
    sent = sent_rows(cap)

    def behind(t, total):
        def test(column, width):
            lane = iota((tile, width), 1)
            if sent < GROUP:
                lane = jnp.where(lane < sent, lane, lane - sent)
            return column == lane + t * GROUP

        return total + group_sum(rank, test, parts, cap, t)

    exposure = lax.fori_loop(0, cap // GROUP, behind, exposure_ref[own, :])
    part = tile // 2
    cuts = [slice(0, part), slice(part, tile)]
    at = [pl.ds(pl.multiple_of(step * tile + k * part, part), part) for k in range(2)]
    etas = []
    for k in range(2):
        start = step * 2 * tile + k * part
        top = weight[pl.ds(pl.multiple_of(start, part), part), :].astype(F32)
        rest = weight[pl.ds(pl.multiple_of(start + tile, part), part), :].astype(F32)
        value = (top + rest) * exposure[cuts[k]] - indicator[at[k], :].astype(F32)
        etas.append(value.astype(BF16))
    mids = [dot(eta, w_out[...], 1, 1) for eta in etas]
    grad_out[...] += dot(hidden[own, :], jnp.concatenate(etas, axis=0), 0, 0)
    mids = [(mids[k] * slope_mid[at[k], :]).astype(BF16) for k in range(2)]
    pres = [dot(mid, w_mid[...], 1, 1) for mid in mids]
    grad_mid[...] += dot(first_hidden[own, :], jnp.concatenate(mids, axis=0), 0, 0)
    pres = [(pres[k] * slope_in[at[k], :]).astype(BF16) for k in range(2)]
    grad_in[...] += dot(x_ref[own, :], jnp.concatenate(pres, axis=0), 0, 0)
    for k in range(2):
        grad_x[cuts[k], :] = dot(pres[k], w_in[...], 1, 1).astype(BF16)

    @pl.when(step == pl.num_programs(0) - 1)
    def _():
        body, rest = grad_mid.shape[0], grad_out.shape[0] // 2
        end = body + rest

        def write(out, block, at):
            out[0:body, :] = block[...] * factor
            out[body:end, :] = grad_out[at : at + rest, :] * factor
            out[end:, :] = note[...] + log_part[...]

        @pl.when(half[0] == 0)
        def _():
            write(keep, grad_mid, 0)
            write(send, grad_in, rest)

        @pl.when(half[0] != 0)
        def _():
            write(keep, grad_in, rest)
            write(send, grad_mid, 0)


def backward(cap, factor, half, rank, exposure, got, notes, kept, features, w_in, w_mid, w_out):
    rows, width = features.shape
    out_width = exposure.shape[1]
    halves = (w_mid.shape[0] + w_out.shape[0] // 2 + 8, out_width)
    tiles = [in_vmem(a) for a in (*kept, features)]
    weights = (w_in, w_mid, w_out)
    return pl.pallas_call(
        partial(backward_kernel, cap, factor),
        grid=(rows // TILE,),
        in_specs=[pl.BlockSpec(memory_space=pltpu.SMEM), lanes_of(1, TILE)]
        + [whole()] * (2 + len(notes))
        + [whole()] * (len(tiles) + 3),
        out_specs=[rows_of(TILE, width), whole(), whole()],
        out_shape=[
            pltpu.HBM((rows, width), BF16), pltpu.HBM(halves, F32),
            jax.ShapeDtypeStruct(halves, F32),
        ],
        scratch_shapes=[pltpu.VMEM((2 * sent_rows(cap), out_width), BF16)]
        + [pltpu.VMEM(w.shape, F32) for w in weights],
        compiler_params=params(20),
        name="backward",
    )(half, rank, in_vmem(exposure), got, *notes, *tiles, *weights)


def in_steps(rows, work):
    step = 16 if rows % 16 == 0 else 8
    if rows <= step:
        work(0, rows)
        return

    def body(k, _):
        work(pl.multiple_of(k * step, 8), step)
        return 0

    lax.fori_loop(0, rows // step, body, 0, unroll=2)


def spread_kernel(sizes, streams, fetch, me, *refs):
    count = sum(sizes)
    outs = iter(refs[count:])
    if fetch:
        held, sems = refs[-1 - count : -1], refs[-1]
        copies = [
            pltpu.make_async_copy(refs[i], held[i], sems.at[i]) for i in range(count)
        ]
        for copy in copies:
            copy.start()
        for copy in copies:
            copy.wait()
        refs = held
    groups_of = []
    for size in sizes:
        groups_of.append(refs[:size])
        refs = refs[size:]

    def total(which, rows):
        value = groups_of[which][0][rows, :]
        for ref in groups_of[which][1:]:
            value = value + ref[rows, :]
        return value

    for i, (which, at, rows, tail_at, tail, groups) in enumerate(streams):
        if not groups:
            flag = jnp.max(total(which, pl.ds(at, rows)))
            next(outs)[0] = jnp.where(flag > 0.0, 1, 0).astype(I32)
            continue
        piece = rows // groups
        for m in range(groups):
            out = next(outs)
            begin = at
            if groups > 1:
                begin = pl.multiple_of(at + jnp.bitwise_xor(me[i], m) * piece, 8)

            def work(row, step, out=out, begin=begin):
                source = pl.ds(pl.multiple_of(begin + row, 8), step)
                out[pl.ds(row, step), :] = total(which, source)

            in_steps(piece, work)
            if tail:
                out[piece : piece + tail, :] = total(which, pl.ds(tail_at, tail))


def spread(terms, streams, me, name, fetch=False):
    width = terms[0][0].shape[1]
    shapes, places = [], []
    for _, _, rows, _, tail, groups in streams:
        if groups:
            shapes += [pltpu.VMEM((rows // groups + tail, width), F32)] * groups
            places += [pl.BlockSpec(memory_space=pltpu.VMEM)] * groups
        else:
            shapes.append(jax.ShapeDtypeStruct((1,), I32))
            places.append(pl.BlockSpec(memory_space=pltpu.SMEM))
    flat = [a for term in terms for a in term]
    scratch = [pltpu.VMEM(a.shape, F32) for a in flat] + [pltpu.SemaphoreType.DMA((len(flat),))]
    out = pl.pallas_call(
        partial(spread_kernel, [len(term) for term in terms], streams, fetch),
        in_specs=[pl.BlockSpec(memory_space=pltpu.SMEM)]
        + [pl.BlockSpec(memory_space=pl.ANY if fetch else pltpu.VMEM)] * len(flat),
        out_specs=places,
        out_shape=shapes,
        scratch_shapes=scratch if fetch else [],
        compiler_params=params(16),
        name=name,
    )(me, *flat)
    parts = []
    for stream in streams:
        parts.append(out[: max(stream[-1], 1)])
        out = out[max(stream[-1], 1) :]
    return parts


def collect_kernel(places, me, *refs):
    count = sum(groups for groups, _, _ in places)
    outs = refs[count:]
    start = 0
    for i, (groups, which, at) in enumerate(places):
        piece = refs[start].shape[0]
        for m in range(groups):
            begin = pl.multiple_of(at + jnp.bitwise_xor(me[i], m) * piece, 8)

            def work(row, step, out=outs[which], ref=refs[start + m], begin=begin):
                target = pl.ds(pl.multiple_of(begin + row, 8), step)
                out[target, :] = ref[pl.ds(row, step), :]

            in_steps(piece, work)
        start += groups


def collect(streams, out_rows, me, name):
    flat = [a for pieces, _, _ in streams for a in pieces]
    width = flat[0].shape[1]
    return pl.pallas_call(
        partial(collect_kernel, [(len(pieces), which, at) for pieces, which, at in streams]),
        in_specs=[pl.BlockSpec(memory_space=pltpu.SMEM)]
        + [pl.BlockSpec(memory_space=pltpu.VMEM)] * len(flat),
        out_specs=[pl.BlockSpec(memory_space=pltpu.VMEM)] * len(out_rows),
        out_shape=[pltpu.VMEM((rows, width), F32) for rows in out_rows],
        compiler_params=params(16),
        name=name,
    )(me, *flat)


def plan(body, rest):
    strata, chain = lax.axis_size("strata"), lax.axis_size("chain")
    if strata % 2 or chain % 4 or strata & (strata - 1) or chain & (chain - 1):
        return None
    across = chain // 4
    plane, line = strata // 2 * across, 4
    if body % (8 * plane * line) or rest % (8 * line):
        return None
    return across, plane, line


def hop(block, strata_flip, chain_flip):
    strata, chain = lax.axis_size("strata"), lax.axis_size("chain")
    route = [
        (s * chain + c, (s ^ strata_flip) * chain + (c ^ chain_flip))
        for s in range(strata)
        for c in range(chain)
    ]
    return lax.ppermute(block, ("strata", "chain"), route)


def hops(groups):
    across, plane, line = groups
    strata, chain = lax.axis_index("strata"), lax.axis_index("chain")

    def plane_hops(pieces):
        return [pieces[0]] + [
            hop(pieces[m], m // across * 2, m % across) for m in range(1, plane)
        ]

    def line_hops(pieces):
        return [pieces[0]] + [hop(pieces[m], 0, m * across) for m in range(1, line)]

    return plane_hops, line_hops, strata // 2 * across + chain % across, chain // across


def reduced(keep, send, body, rest, groups):
    plane_hops, line_hops, in_plane, in_line = hops(groups)
    _, plane, line = groups
    end = body + rest
    tail = keep.shape[0] - end
    a, b = spread(
        [[in_hbm(keep), hop(send, 1, 0)]],
        [(0, 0, body, end, tail, plane), (0, body, rest, 0, 0, line)],
        jnp.stack([in_plane, in_line]), "spread_first", fetch=True,
    )
    a, b = plane_hops(a), line_hops(b)
    size_a, size_b = body // plane, rest // line
    none = jnp.zeros((3,), I32)
    ((b,),) = spread([b], [(0, 0, size_b, 0, 0, 1)], none, "lines_summed")
    (a,) = spread(
        [a], [(0, 0, size_a, size_a, tail, line)], in_line.reshape(1), "spread_second"
    )
    a, b = line_hops(a), plane_hops([b] * plane)
    ((b,),) = spread([b], [(0, 0, size_b, 0, 0, 1)], none, "rest_summed")
    size_a = size_a // line
    (a,), (note,) = spread(
        [a], [(0, 0, size_a, 0, 0, 1), (0, size_a, tail, 0, 0, 1)], none, "body_summed"
    )
    ((flag,),) = spread([[note]], [(0, 1, 1, 0, 0, 0)], none, "flag")
    (a,) = collect(
        [(line_hops([a] * line), 0, 0)], [body // plane], in_line.reshape(1), "collect_first"
    )
    return flag, note, a, b


def gathered(a, b, body, rest, groups):
    plane_hops, line_hops, in_plane, in_line = hops(groups)
    _, plane, line = groups
    a, b = plane_hops([a] * plane), line_hops([b] * line)
    (own,) = collect(
        [(a, 0, 0), (b, 0, body)], [body + rest], jnp.stack([in_plane, in_line]), "collect_second"
    )
    return own, hop(own, 1, 0)


def place_kernel(of_core, half, block, *refs):
    grad_in, grad_mid, grad_out, sems = refs[-4:]
    body, rest = grad_mid.shape[0], grad_out.shape[0] // 2

    def write(target, at):
        copies = [
            pltpu.make_async_copy(block.at[pl.ds(0, body)], target, sems.at[0]),
            pltpu.make_async_copy(
                block.at[pl.ds(body, rest)], grad_out.at[pl.ds(at, rest)], sems.at[1]
            ),
        ]
        for copy in copies:
            copy.start()
        for copy in copies:
            copy.wait()

    @pl.when(half[0] == of_core)
    def _():
        write(grad_mid, 0)

    @pl.when(half[0] != of_core)
    def _():
        write(grad_in, rest)


def place(of_core, half, block, shapes, results):
    somewhere = pl.BlockSpec(memory_space=pl.ANY)
    return pl.pallas_call(
        partial(place_kernel, of_core),
        in_specs=[
            pl.BlockSpec(memory_space=pltpu.SMEM), pl.BlockSpec(memory_space=pltpu.VMEM)
        ]
        + [somewhere] * len(results),
        out_specs=[somewhere] * 3,
        out_shape=[pltpu.HBM(shape, F32) for shape in shapes],
        scratch_shapes=[pltpu.SemaphoreType.DMA((2,))],
        input_output_aliases={2 + i: i for i in range(len(results))},
        compiler_params=params(16),
        name="place",
    )(half, block, *results)


def finish(half, own, got, shapes):
    results = place(0, half, own, shapes, ())
    return place(1, half, got, shapes, results)


def from_behind(block, axis, distance):
    devices = range(lax.axis_size(axis))
    route = [(i - distance, i) for i in devices if i - distance in devices]
    return lax.ppermute(block, axis, route)


def pipeline(cap, total_rows, half, features, events, tie_first, entry_row, w_in, w_mid, w_out):
    rows = features.shape[0]
    block_start = (lax.axis_index("chain") * rows).reshape(1)
    first = tie_first - block_start
    entry = entry_row - block_start
    first_line = first.reshape(1, rows)
    entry_line = entry.reshape(1, rows)
    starts = first[::LANES]
    (
        first_hidden, hidden, slope_in, slope_mid, indicator, weight, send, note, rank,
    ) = trunk(
        cap, block_start, entry_row.reshape(1, rows), features, events, w_in, w_mid, w_out
    )
    got = from_behind(send, "chain", -1)
    risk = own_risk(starts, entry_line, first_line, weight)
    hazard, sums = hazards(cap, first_line, risk, indicator, got)
    got_sums = from_behind(sums, "chain", 1)
    exposure, log_part = own_exposure(starts, first_line, entry_line, hazard)
    kept = (weight, indicator, hidden, slope_mid, first_hidden, slope_in)
    return backward(
        cap, total_rows ** (-0.5), half, rank, exposure, got_sums, (note, log_part), kept,
        features, w_in, w_mid, w_out,
    )


def on_device(features, events, tie_first, entry_row, w_in, w_mid, w_out):
    rows = features.shape[0]
    total_rows = rows * lax.axis_size("chain") * lax.axis_size("strata")
    args = (features, events, tie_first, entry_row, w_in, w_mid, w_out)
    shapes = (w_in.shape, w_mid.shape, w_out.shape)
    body, rest = w_mid.shape[0], w_out.shape[0] // 2
    end = body + rest
    groups = plan(body, rest)
    half = jnp.zeros((1,), I32)
    if groups:
        half = half + lax.axis_index("strata") % 2

    def run(cap):
        grad_x, keep, send = pipeline(cap, total_rows, half, *args)
        if groups:
            flag, note, a, b = reduced(keep, send, body, rest, groups)
        else:
            a, b = lax.psum((keep, send[:end]), ("strata", "chain"))
            a, note = a[:end], a[end:]
            flag = (note[1, 0:1] > 0).astype(I32)
        return flag, note, grad_x, a, b

    _, note, grad_x, a, b = lax.while_loop(
        lambda state: state[0][0] > 0, lambda _: run(rows), run(min(GROUP, rows))
    )
    own, other = gathered(a, b, body, rest, groups) if groups else (a, b)
    return (note[0] / total_rows, grad_x, *finish(half, own, other, shapes))


def solution(mesh):
    placed = (
        P(("strata", "chain"), None),
        P(("strata", "chain"), None),
        P(("strata", "chain")),
        P(("strata", "chain")),
        P(),
        P(),
        P(),
    )
    return jax.shard_map(
        on_device,
        mesh=mesh,
        in_specs=placed,
        out_specs=(P(), P(("strata", "chain"), None), P(), P(), P()),
        check_vma=False,
    )
```
